128 devices in a mesh: seq: 64 (over y, x, z), head: 2 (over core).
Axes of the slice: x: 4, y: 4, z: 4, core: 2. Of those that a mesh axis runs over, the one named last changes fastest.
Arguments:
- queries: bfloat16 [8192, 80, 576], P('seq', 'head'), may hold values from -117 to 117
- latent: bfloat16 [8192, 576], P('seq'), may hold values from -6 to 6
- d_out: bfloat16 [8192, 80, 512], P('seq', 'head'), may hold values from -6 to 6
- index_q: bfloat16 [8192, 64, 128], P('seq', 'head'), may hold values from -8 to 8
- index_w: bfloat16 [8192, 64], P('seq', 'head'), may hold values from -4 to 4
- index_k: bfloat16 [8192, 128], P('seq'), may hold values from -6 to 6
- picks: int32 [8192, 4], P('seq'), may hold values from -1 to 63, as said below
Outputs:
- d_queries: bfloat16 [8192, 80, 576], P('seq', 'head')
- d_latent: bfloat16 [8192, 576], P('seq')
- d_index_q: bfloat16 [8192, 64, 128], P('seq', 'head')
- d_index_w: float32 [8192, 64], P('seq', 'head')
- d_index_k: bfloat16 [8192, 128], P('seq')
The draws below stay inside these ranges and needn't reach their ends.
Inputs may be any that keep to these rules, and one draw needn't show every extreme that they name: `picks`: row t lists first its own block b = t // 128, then block 0 if b > 0, then 4 - 2 further distinct blocks among 1 to b - 1; slots without a block hold -1, so a row lists min(4, b + 1) distinct blocks.
All inputs are finite; a program needn't handle non-finite values.
Results may differ from the reference program's by a relative error of at most 0.038.
Values may be sent and summed in bfloat16 or wider, within the bound.
No kernel may reach another device: no remote copies, remote signals or barrier semaphores. Data moves between devices by JAX's collectives and lax.ppermute only.
A program may use at most 256 MiB of HBM per device.

```python
import jax
import jax.numpy as jnp
from jax import lax

BLOCK = 128
PICK = 4
H = 80
D_LAT = 576
D_V = 512
IH = 64
ID = 128
TOKENS = 8192


def latent_base(key):
    gauss = jnp.clip(jax.random.normal(jax.random.fold_in(key, 101), (TOKENS, D_LAT), jnp.float32), -6.0, 6.0)
    return gauss


def index_base(key):
    gauss = jnp.clip(jax.random.normal(jax.random.fold_in(key, 103), (TOKENS, ID), jnp.float32), -6.0, 6.0)
    return gauss


def draw_latent(key, part):
    base = latent_base(key)
    return base.astype(jnp.bfloat16)


def draw_index_k(key, part):
    base = index_base(key)
    return base.astype(jnp.bfloat16)


def draw_queries(key, part):
    key = jax.random.fold_in(key, 12)
    vals = jnp.clip(jax.random.normal(key, (TOKENS, H, D_LAT), jnp.float32), -6.0, 6.0)
    return vals.astype(jnp.bfloat16)


def draw_index_q(key, part):
    key = jax.random.fold_in(key, 14)
    vals = 0.25 * jnp.clip(jax.random.normal(key, (TOKENS, IH, ID), jnp.float32), -6.0, 6.0)
    return vals.astype(jnp.bfloat16)


def draw_index_w(key, part):
    key = jax.random.fold_in(key, 15)
    vals = jnp.clip(jax.random.normal(key, (TOKENS, IH), jnp.float32), -4.0, 4.0)
    return vals.astype(jnp.bfloat16)


def draw_picks(key, part):
    key = jax.random.fold_in(key, 17)
    nblk = TOKENS // BLOCK
    own = jnp.arange(TOKENS, dtype=jnp.int32) // BLOCK
    blocks = jnp.arange(nblk, dtype=jnp.int32)
    noise = jax.random.randint(key, (TOKENS, nblk), 0, 64, dtype=jnp.int32)
    recent = (blocks[None, :] >= own[:, None] - 3).astype(jnp.int32) * 40
    score = (noise + recent) * nblk + blocks[None, :]
    usable = (blocks[None, :] >= 1) & (blocks[None, :] < own[:, None])
    score = jnp.where(usable, score, -1)
    best = lax.top_k(score, PICK - 2)[0]
    rest = jnp.where(best >= 0, best % nblk, -1)
    sink = jnp.where(own > 0, 0, -1)
    return jnp.concatenate([own[:, None], sink[:, None], rest], axis=1).astype(jnp.int32)


def level_of(rng, shape, pieces, smallest, largest):
    loudness = 1.0
    for axis_at, shards_of in pieces:
        draws = jax.random.uniform(jax.random.fold_in(jax.random.fold_in(rng, 6), axis_at), (shards_of,), jnp.float32, smallest / len(pieces), largest / len(pieces))
        loudness = loudness * jnp.repeat(jnp.exp(draws), shape[axis_at] // shards_of).reshape((-1,) + (1,) * (len(shape) - 1 - axis_at))
    return loudness


def normal_values(stream_key, shape, deviation, limit, split=(), held_as=jnp.bfloat16):
    drawn = jax.random.normal(stream_key, shape, jnp.float32) * deviation
    if len(split) > 0:
        drawn = level_of(stream_key, shape, split, -0.22, 0.18) * drawn
    return jnp.clip(drawn, min=-limit, max=limit).astype(held_as)


def setup_inputs(seed: int = 0) -> dict:
    key_of = jax.random.split(jax.random.key(seed), 8)
    return {
        "queries": draw_queries(jax.random.fold_in(key_of[7], 71), 0),
        "latent": draw_latent(jax.random.fold_in(key_of[7], 71), 0),
        "d_out": normal_values(key_of[2], (TOKENS, H, D_V), 1.0, 6.0, ((0, 64), (1, 2))),
        "index_q": draw_index_q(jax.random.fold_in(key_of[7], 71), 0),
        "index_w": draw_index_w(jax.random.fold_in(key_of[7], 71), 0),
        "index_k": draw_index_k(jax.random.fold_in(key_of[7], 71), 0),
        "picks": draw_picks(jax.random.fold_in(key_of[7], 71), 0),
    }


softmax_scale = 192.0 ** -0.5
kl_weight = 32.0
neg_large = -1.0e30


def masked_softmax(scores, allowed):
    masked = jnp.where(allowed, scores, neg_large)
    top = jnp.max(masked, axis=-1, keepdims=True)
    expo = jnp.where(allowed, jnp.exp(masked - top), 0.0)
    return expo / jnp.sum(expo, axis=-1, keepdims=True)


def reference(queries, latent, d_out, index_q, index_w, index_k, picks):
    nblk = TOKENS // BLOCK
    span = PICK * BLOCK
    inv_root = IH ** -0.5
    lat_blocks = latent.reshape(nblk, BLOCK, D_LAT)
    ik_blocks = index_k.reshape(nblk, BLOCK, ID)
    offsets = jnp.arange(BLOCK, dtype=jnp.int32)

    def step(carry, blockno):
        acc_lat, acc_ik = carry
        first = (blockno * BLOCK).astype(jnp.int32)
        q_grp = lax.dynamic_slice_in_dim(queries, first, BLOCK, 0).astype(jnp.float32)
        do_grp = lax.dynamic_slice_in_dim(d_out, first, BLOCK, 0).astype(jnp.float32)
        iq_grp = lax.dynamic_slice_in_dim(index_q, first, BLOCK, 0).astype(jnp.float32)
        iw_grp = lax.dynamic_slice_in_dim(index_w, first, BLOCK, 0).astype(jnp.float32)
        chosen = lax.dynamic_slice_in_dim(picks, first, BLOCK, 0)
        blk = jnp.maximum(chosen, 0).astype(jnp.int32)
        kpos = (blk[:, :, None] * BLOCK + offsets).reshape(BLOCK, span)
        qpos = first + offsets
        allowed = jnp.repeat(chosen >= 0, BLOCK, axis=1) & (kpos <= qpos[:, None])
        keys = lat_blocks[blk].reshape(BLOCK, span, D_LAT).astype(jnp.float32)
        scores = jnp.einsum('thd,tsd->ths', q_grp, keys) * softmax_scale
        probs = masked_softmax(scores, allowed[:, None, :])
        dprob = jnp.einsum('thv,tsv->ths', do_grp, keys[:, :, :D_V])
        delta = jnp.sum(probs * dprob, axis=2, keepdims=True)
        dscore = (probs * (dprob - delta) * softmax_scale).astype(jnp.bfloat16).astype(jnp.float32)
        probs_low = probs.astype(jnp.bfloat16).astype(jnp.float32)
        d_q = jnp.einsum('ths,tsd->thd', dscore, keys).astype(jnp.bfloat16)
        d_k = jnp.einsum('ths,thd->tsd', dscore, q_grp)
        d_v = jnp.einsum('ths,thv->tsv', probs_low, do_grp)
        d_lat = d_k + jnp.pad(d_v, ((0, 0), (0, 0), (0, D_LAT - D_V)))
        target = jnp.sum(probs, axis=1) / H
        iks = ik_blocks[blk].reshape(BLOCK, span, ID).astype(jnp.float32)
        gate = jnp.einsum('tjd,tsd->tjs', iq_grp, iks)
        soft_gate = jax.nn.softplus(gate)
        logits = jnp.sum(iw_grp[:, :, None] * soft_gate, axis=1) * inv_root
        soft = masked_softmax(logits, allowed)
        d_logit = jnp.where(allowed, kl_weight * (soft - target), 0.0)
        d_w = jnp.sum(d_logit[:, None, :] * soft_gate, axis=2) * inv_root
        d_gate = (d_logit[:, None, :] * iw_grp[:, :, None] * jax.nn.sigmoid(gate) * inv_root).astype(jnp.bfloat16).astype(jnp.float32)
        d_iq = jnp.einsum('tjs,tsd->tjd', d_gate, iks).astype(jnp.bfloat16)
        d_ik = jnp.einsum('tjs,tjd->tsd', d_gate, iq_grp)
        acc_lat = acc_lat.at[blk].add(d_lat.reshape(BLOCK, PICK, BLOCK, D_LAT))
        acc_ik = acc_ik.at[blk].add(d_ik.reshape(BLOCK, PICK, BLOCK, ID))
        return (acc_lat, acc_ik), (d_q, d_iq, d_w)

    start = (jnp.zeros((nblk, BLOCK, D_LAT), jnp.float32), jnp.zeros((nblk, BLOCK, ID), jnp.float32))
    (acc_lat, acc_ik), (d_q, d_iq, d_w) = lax.scan(step, start, jnp.arange(nblk, dtype=jnp.int32))
    d_queries = d_q.reshape(TOKENS, H, D_LAT)
    d_latent = acc_lat.reshape(TOKENS, D_LAT).astype(jnp.bfloat16)
    d_index_q = d_iq.reshape(TOKENS, IH, ID)
    d_index_w = d_w.reshape(TOKENS, IH)
    d_index_k = acc_ik.reshape(TOKENS, ID).astype(jnp.bfloat16)
    return (d_queries, d_latent, d_index_q, d_index_w, d_index_k)
```

```python
import functools

import jax
import jax.numpy as jnp
from jax import lax
from jax.experimental import pallas as pl
from jax.experimental.pallas import tpu as pltpu
from jax.sharding import PartitionSpec as P

BLOCK = 128
PICK = 4
H = 80
IH = 64
LANES = 128

softmax_scale = 192.0 ** (-0.5)
kl_weight = 32.0
neg_large = -1e30
inv_root = IH ** (-0.5)

G_ATT = 8
G_IDX = 8
PAIRS = 4
HALF = BLOCK // 2
VMEM_LIMIT = 58 * 1024 * 1024


def dot(a, b, ca, cb):
    return lax.dot_general(a, b, (((ca,), (cb,)), ((), ())), preferred_element_type=jnp.float32)


def mask_row(picks_ref, t, tloc):
    lane = lax.broadcasted_iota(jnp.int32, (1, LANES), 1)
    parts = [jnp.where(lane <= tloc, 0.0, neg_large)]
    for j in range(1, PICK):
        parts.append(jnp.where(lane + picks_ref[t * PICK + j] * LANES >= 0, 0.0, neg_large))
    return jnp.concatenate(parts, axis=1)


def block_of(keys, b):
    return keys[pl.ds(2 * b, 2)].reshape(BLOCK, keys.shape[2])


def load_keys(lat_ref, keys, tails, sem):
    full = keys.shape[2] // LANES - 1
    copies = [
        pltpu.make_async_copy(
            lat_ref.at[:, pl.ds((c + 1) * HALF, HALF), :],
            keys.at[:, :, pl.ds(c * LANES, LANES)],
            sem.at[c],
        )
        for c in range(full)
    ]
    copies.append(
        pltpu.make_async_copy(
            lat_ref.at[:, pl.ds((full + 1) * HALF, HALF // 2), :], tails, sem.at[full]
        )
    )
    for cp in copies:
        cp.start()

    def finish():
        for cp in copies:
            cp.wait()

        def unpack(i, carry):
            low = tails[i]
            high = pltpu.roll(low.astype(jnp.float32), HALF, 1).astype(jnp.bfloat16)
            keys[i, :, pl.ds(full * LANES, LANES)] = jnp.concatenate([low, high], axis=0)
            return carry

        lax.fori_loop(0, keys.shape[0], unpack, 0, unroll=4)

    return finish


def attend_kernel(
    groups, heads, picks_ref, own_ref, tile_ref, pair_ref, stk_hbm, lat_ref,
    dsx_ref, dsh_ref, tgt_ref, keep_ref, send_ref,
    keys, tails, stk, extra, acc, acc_sh, sem,
):
    step = pl.program_id(0)
    own = own_ref[0]
    core = own_ref[1]
    rows = 2 * heads
    nblk = acc.shape[0]
    tokens = stk.shape[0]
    full = keys.shape[2] // LANES - 1

    @pl.when(step == 0)
    def _():
        load_stk = pltpu.make_async_copy(stk_hbm, stk, sem.at[full + 1])
        finish = load_keys(lat_ref, keys, tails, sem)
        load_stk.start()

        def zero(b, carry):
            acc[b] = jnp.zeros(acc.shape[1:], jnp.float32)
            return carry

        lax.fori_loop(0, nblk, zero, 0)
        acc_sh[...] = jnp.zeros(acc_sh.shape, jnp.float32)
        finish()
        load_stk.wait()

        def tile_pair(i, carry):
            for u in range(2):
                tile = 2 * i + u
                pairs = [pair_ref[tile * PAIRS + k] for k in range(PAIRS)]
                lhs = jnp.concatenate([stk[jnp.minimum(p // 2, tokens - 1)] for p in pairs], axis=0)
                out = dot(lhs, block_of(keys, tile_ref[1 + tile]), 1, 1)
                for k, p in enumerate(pairs):
                    extra[p] = out[k * rows : (k + 1) * rows]
            return carry

        lax.fori_loop(0, tile_ref[0], tile_pair, 0)

    ksh = jnp.concatenate([block_of(keys, own), block_of(keys, 0)], axis=0)
    stk_all = stk[pl.ds(step * groups, groups)].reshape(groups * rows, stk.shape[2])
    both_sh = dot(stk_all, ksh, 1, 1)
    ds_list, gr_list, tgt_list = [], [], []
    for g in range(groups):
        t = step * groups + g
        e0 = jnp.maximum(picks_ref[t * PICK + 2], 0)
        e1 = jnp.maximum(picks_ref[t * PICK + 3], 0)
        bias = mask_row(picks_ref, t, t)
        both_x = jnp.concatenate([extra[2 * t], extra[2 * t + 1]], axis=1)
        lo = g * rows
        scores = jnp.concatenate([both_sh[lo : lo + heads], both_x[:heads]], axis=1)
        dprob = jnp.concatenate([both_sh[lo + heads : lo + rows], both_x[heads:]], axis=1)
        scores = scores * softmax_scale + bias
        top = jnp.max(scores, axis=1, keepdims=True)
        expo = jnp.exp(scores - top)
        probs = expo * (1.0 / jnp.sum(expo, axis=1, keepdims=True))
        delta = jnp.sum(probs * dprob, axis=1, keepdims=True)
        dscore = probs * (dprob - delta) * softmax_scale
        tgt_list.append(jnp.sum(probs, axis=0, keepdims=True))
        grads = jnp.concatenate([dscore, probs], axis=0).astype(jnp.bfloat16)
        dsx_ref[2 * g] = dscore[:, 2 * BLOCK : 3 * BLOCK]
        dsx_ref[2 * g + 1] = dscore[:, 3 * BLOCK :]
        upd = dot(grads[:, 2 * BLOCK :], stk[t], 0, 0)
        acc[e0] += upd[:BLOCK]
        acc[e1] += upd[BLOCK:]
        ds_list.append(dscore[:, : 2 * BLOCK])
        gr_list.append(grads[:, : 2 * BLOCK])
    dsh_ref[...] = jnp.concatenate(ds_list, axis=0).astype(jnp.bfloat16)
    acc_sh[...] += dot(jnp.concatenate(gr_list, axis=0), stk_all, 0, 0)
    tgt_ref[...] = jnp.concatenate(tgt_list, axis=0)

    @pl.when(step == pl.num_programs(0) - 1)
    def _():
        acc[own] += acc_sh[pl.ds(0, BLOCK), :]
        acc[0] += acc_sh[pl.ds(BLOCK, BLOCK), :]

        def cast(b, carry):
            for k, which in enumerate((core, 1 - core)):
                part = acc[b, pl.ds(pl.multiple_of(which * HALF, HALF), HALF), :]
                keys[k * nblk + b] = part.astype(jnp.bfloat16)
                last = part[:, full * LANES :]
                packed = last[: HALF // 2] + pltpu.roll(last[HALF // 2 :], HALF, 1)
                tails[k * nblk + b] = packed.astype(jnp.bfloat16)
            return carry

        lax.fori_loop(0, nblk, cast, 0)
        stores = []
        for k, ref in enumerate((keep_ref, send_ref)):
            part = pl.ds(k * nblk, nblk)
            for c in range(full):
                stores.append(
                    pltpu.make_async_copy(
                        keys.at[part, :, pl.ds(c * LANES, LANES)],
                        ref.at[:, pl.ds(c * HALF, HALF), :],
                        sem.at[k * (full + 1) + c],
                    )
                )
            stores.append(
                pltpu.make_async_copy(
                    tails.at[part],
                    ref.at[:, pl.ds(full * HALF, HALF // 2), :],
                    sem.at[k * (full + 1) + full],
                )
            )
        for cp in stores:
            cp.start()
        for cp in stores:
            cp.wait()


def attend_call(picks, own, tiles, pairs, stk, gathered, heads):
    tokens, rows, width = stk.shape
    nblk = gathered.shape[0] // 2
    full = width // LANES - 1
    groups = G_ATT
    packed = full * HALF + HALF // 2
    return pl.pallas_call(
        functools.partial(attend_kernel, groups, heads),
        grid_spec=pltpu.PrefetchScalarGridSpec(
            num_scalar_prefetch=4,
            grid=(tokens // groups,),
            in_specs=[pl.BlockSpec(memory_space=pl.ANY), pl.BlockSpec(memory_space=pl.ANY)],
            out_specs=[
                pl.BlockSpec((2 * groups, heads, BLOCK), lambda i, *_: (i, 0, 0)),
                pl.BlockSpec((groups * heads, 2 * BLOCK), lambda i, *_: (i, 0)),
                pl.BlockSpec((groups, PICK * BLOCK), lambda i, *_: (i, 0)),
                pl.BlockSpec(memory_space=pl.ANY),
                pl.BlockSpec(memory_space=pl.ANY),
            ],
            scratch_shapes=[
                pltpu.VMEM((2 * nblk, HALF, width), jnp.bfloat16),
                pltpu.VMEM((2 * nblk, HALF // 2, LANES), jnp.bfloat16),
                pltpu.VMEM((tokens, rows, width), jnp.bfloat16),
                pltpu.VMEM((2 * tokens + 1, rows, BLOCK), jnp.float32),
                pltpu.VMEM((nblk, BLOCK, width), jnp.float32),
                pltpu.VMEM((2 * BLOCK, width), jnp.float32),
                pltpu.SemaphoreType.DMA((2 * full + 2,)),
            ],
        ),
        out_shape=[
            jax.ShapeDtypeStruct((2 * tokens, heads, BLOCK), jnp.float32),
            jax.ShapeDtypeStruct((tokens * heads, 2 * BLOCK), jnp.bfloat16),
            jax.ShapeDtypeStruct((tokens, PICK * BLOCK), jnp.float32),
            jax.ShapeDtypeStruct((nblk, packed, LANES), jnp.bfloat16),
            jax.ShapeDtypeStruct((nblk, packed, LANES), jnp.bfloat16),
        ],
        compiler_params=pltpu.CompilerParams(vmem_limit_bytes=VMEM_LIMIT),
        cost_estimate=pl.CostEstimate(
            flops=60_000_000_000, bytes_accessed=50_000_000, transcendentals=3_000_000
        ),
        name="attend",
    )(picks, own, tiles, pairs, stk, gathered)


def query_grad_kernel(groups, heads, own_ref, tile_ref, pair_ref, dsx_ref, dsh_ref, lat_ref, dq_ref, keys, tails, total, sem):
    own = own_ref[0]
    npairs = dsx_ref.shape[0]
    width = keys.shape[2]
    finish = load_keys(lat_ref, keys, tails, sem)

    def zero(t, carry):
        total[t] = jnp.zeros(total.shape[1:], jnp.float32)
        return carry

    lax.fori_loop(0, total.shape[0], zero, 0)
    finish()

    def tile_pair(i, carry):
        for u in range(2):
            tile = 2 * i + u
            pairs = [pair_ref[tile * PAIRS + k] for k in range(PAIRS)]
            lhs = jnp.concatenate([dsx_ref[jnp.minimum(p, npairs - 1)] for p in pairs], axis=0)
            out = dot(lhs.astype(jnp.bfloat16), block_of(keys, tile_ref[1 + tile]), 1, 0)
            for k, p in enumerate(pairs):
                total[p // 2] += out[k * heads : (k + 1) * heads]
        return carry

    lax.fori_loop(0, tile_ref[0], tile_pair, 0)
    ksh = jnp.concatenate([block_of(keys, own), block_of(keys, 0)], axis=0)

    def shared(i, carry):
        part = pl.ds(pl.multiple_of(i * groups * heads, groups * heads), groups * heads)
        out = dot(dsh_ref[part, :], ksh, 1, 0)
        out = out + total[pl.ds(i * groups, groups)].reshape(groups * heads, width)
        dq_ref[part, :] = out.astype(jnp.bfloat16)
        return carry

    lax.fori_loop(0, dsh_ref.shape[0] // (groups * heads), shared, 0)


def query_grad_call(own, tiles, pairs, dsx, dsh, gathered, heads, width):
    tokens = dsx.shape[0] // 2
    nblk = gathered.shape[0] // 2
    full = width // LANES - 1
    vmem = pl.BlockSpec(memory_space=pltpu.VMEM)
    smem = pl.BlockSpec(memory_space=pltpu.SMEM)
    return pl.pallas_call(
        functools.partial(query_grad_kernel, G_ATT, heads),
        in_specs=[smem, smem, smem, vmem, vmem, pl.BlockSpec(memory_space=pl.ANY)],
        out_specs=vmem,
        out_shape=jax.ShapeDtypeStruct((tokens * heads, width), jnp.bfloat16),
        scratch_shapes=[
            pltpu.VMEM((2 * nblk, HALF, width), jnp.bfloat16),
            pltpu.VMEM((2 * nblk, HALF // 2, LANES), jnp.bfloat16),
            pltpu.VMEM((tokens + 1, heads, width), jnp.float32),
            pltpu.SemaphoreType.DMA((full + 1,)),
        ],
        compiler_params=pltpu.CompilerParams(vmem_limit_bytes=VMEM_LIMIT),
        cost_estimate=pl.CostEstimate(
            flops=12_000_000_000, bytes_accessed=25_000_000, transcendentals=0
        ),
        name="query_grad",
    )(own, tiles, pairs, dsx, dsh, gathered)


def softplus(x):
    return jnp.maximum(x, 0.0) + jnp.log(1.0 + jnp.exp(-jnp.abs(x)))


def weight_column(wt, t):
    lane = lax.broadcasted_iota(jnp.int32, wt.shape, 1)
    return jnp.sum(jnp.where(lane == t, wt, 0.0), axis=1, keepdims=True)


def index_logits_kernel(groups, heads, picks_ref, own_ref, iq_ref, wt_ref, ik_ref, out_ref):
    step = pl.program_id(0)
    own = own_ref[0]
    ksh = jnp.concatenate([block_of(ik_ref, own), block_of(ik_ref, 0)], axis=0)
    gate_sh = dot(iq_ref[...], ksh, 1, 1)
    wt = wt_ref[...]
    outs = []
    for g in range(groups):
        t = step * groups + g
        e0 = jnp.maximum(picks_ref[t * PICK + 2], 0)
        e1 = jnp.maximum(picks_ref[t * PICK + 3], 0)
        kx = jnp.concatenate([block_of(ik_ref, e0), block_of(ik_ref, e1)], axis=0)
        gate_x = dot(iq_ref[pl.ds(g * heads, heads), :], kx, 1, 1)
        gate = jnp.concatenate([gate_sh[g * heads : (g + 1) * heads], gate_x], axis=1)
        w = weight_column(wt, t)
        outs.append(jnp.sum(w * softplus(gate), axis=0, keepdims=True))
    out_ref[...] = jnp.concatenate(outs, axis=0) * inv_root


def index_back_kernel(
    groups, heads, picks_ref, own_ref, iq_ref, wt_ref, ik_ref, logit_ref, tgt_ref, diq_ref, dwt_ref, dik_ref, acc, acc_sh
):
    step = pl.program_id(0)
    own = own_ref[0]

    @pl.when(step == 0)
    def _():
        acc[...] = jnp.zeros(acc.shape, jnp.float32)
        acc_sh[...] = jnp.zeros(acc_sh.shape, jnp.float32)
        dwt_ref[...] = jnp.zeros(dwt_ref.shape, jnp.float32)

    bias = jnp.concatenate(
        [mask_row(picks_ref, step * groups + g, step * groups + g) for g in range(groups)], axis=0
    )
    logits = logit_ref[...] + bias
    top = jnp.max(logits, axis=1, keepdims=True)
    expo = jnp.exp(logits - top)
    soft = expo * (1.0 / jnp.sum(expo, axis=1, keepdims=True))
    d_logit_all = jnp.where(bias == 0.0, kl_weight * (soft - tgt_ref[...] * (1.0 / H)), 0.0)

    ksh = jnp.concatenate([block_of(ik_ref, own), block_of(ik_ref, 0)], axis=0)
    gate_sh = dot(iq_ref[...], ksh, 1, 1)
    wt = wt_ref[...]
    lane = lax.broadcasted_iota(jnp.int32, wt.shape, 1)
    dwt = dwt_ref[...]
    dg_list, dx_list = [], []
    for g in range(groups):
        t = step * groups + g
        e0 = jnp.maximum(picks_ref[t * PICK + 2], 0)
        e1 = jnp.maximum(picks_ref[t * PICK + 3], 0)
        kx = jnp.concatenate([block_of(ik_ref, e0), block_of(ik_ref, e1)], axis=0)
        iq_g = iq_ref[pl.ds(g * heads, heads), :]
        gate_x = dot(iq_g, kx, 1, 1)
        gate = jnp.concatenate([gate_sh[g * heads : (g + 1) * heads], gate_x], axis=1)
        w = weight_column(wt, t)
        d_logit = d_logit_all[g : g + 1]
        small = jnp.exp(-jnp.abs(gate))
        denom = 1.0 + small
        soft_gate = jnp.maximum(gate, 0.0) + jnp.log(denom)
        sig = jnp.where(gate >= 0.0, 1.0, small) / denom
        dw = jnp.sum(d_logit * soft_gate, axis=1, keepdims=True) * inv_root
        dwt = jnp.where(lane == t, dw, dwt)
        d_gate = (d_logit * (w * inv_root) * sig).astype(jnp.bfloat16)
        gx = d_gate[:, 2 * BLOCK :]
        dx_list.append(dot(gx, kx, 1, 0))
        upd = dot(gx, iq_g, 0, 0)
        acc[e0] += upd[:BLOCK]
        acc[e1] += upd[BLOCK:]
        dg_list.append(d_gate[:, : 2 * BLOCK])
    dwt_ref[...] = dwt
    dg_sh = jnp.concatenate(dg_list, axis=0)
    diq = dot(dg_sh, ksh, 1, 0) + jnp.concatenate(dx_list, axis=0)
    diq_ref[...] = diq.astype(jnp.bfloat16)
    acc_sh[...] += dot(dg_sh, iq_ref[...], 0, 0)

    @pl.when(step == pl.num_programs(0) - 1)
    def _():
        acc[own] += acc_sh[pl.ds(0, BLOCK), :]
        acc[0] += acc_sh[pl.ds(BLOCK, BLOCK), :]
        dik_ref[...] = acc[...].astype(jnp.bfloat16)


def index_logits_call(picks, own, iq, wt, gathered, heads, tokens):
    groups = G_IDX
    span = PICK * BLOCK
    return pl.pallas_call(
        functools.partial(index_logits_kernel, groups, heads),
        grid_spec=pltpu.PrefetchScalarGridSpec(
            num_scalar_prefetch=2,
            grid=(tokens // groups,),
            in_specs=[
                pl.BlockSpec((groups * heads, iq.shape[1]), lambda i, *_: (i, 0)),
                pl.BlockSpec(wt.shape, lambda i, *_: (0, 0)),
                pl.BlockSpec((gathered.shape[0], HALF, LANES), lambda i, *_: (0, 0, 0)),
            ],
            out_specs=pl.BlockSpec((groups, span), lambda i, *_: (i, 0)),
        ),
        out_shape=jax.ShapeDtypeStruct((tokens, span), jnp.float32),
        compiler_params=pltpu.CompilerParams(vmem_limit_bytes=VMEM_LIMIT),
        cost_estimate=pl.CostEstimate(
            flops=10_000_000_000, bytes_accessed=4_000_000, transcendentals=6_000_000
        ),
        name="index_logits",
    )(picks, own, iq, wt, gathered)


def index_back_call(picks, own, iq, wt, gathered, logits, target, heads, tokens):
    groups = G_IDX
    span = PICK * BLOCK
    width = iq.shape[1]
    nblk = gathered.shape[0] // 2
    return pl.pallas_call(
        functools.partial(index_back_kernel, groups, heads),
        grid_spec=pltpu.PrefetchScalarGridSpec(
            num_scalar_prefetch=2,
            grid=(tokens // groups,),
            in_specs=[
                pl.BlockSpec((groups * heads, width), lambda i, *_: (i, 0)),
                pl.BlockSpec(wt.shape, lambda i, *_: (0, 0)),
                pl.BlockSpec((gathered.shape[0], HALF, LANES), lambda i, *_: (0, 0, 0)),
                pl.BlockSpec((groups, span), lambda i, *_: (i, 0)),
                pl.BlockSpec((groups, span), lambda i, *_: (i, 0)),
            ],
            out_specs=[
                pl.BlockSpec((groups * heads, width), lambda i, *_: (i, 0)),
                pl.BlockSpec((heads, tokens), lambda i, *_: (0, 0)),
                pl.BlockSpec((nblk, BLOCK, width), lambda i, *_: (0, 0, 0)),
            ],
            scratch_shapes=[
                pltpu.VMEM((nblk, BLOCK, width), jnp.float32),
                pltpu.VMEM((2 * BLOCK, width), jnp.float32),
            ],
        ),
        out_shape=[
            jax.ShapeDtypeStruct((tokens * heads, width), jnp.bfloat16),
            jax.ShapeDtypeStruct((heads, tokens), jnp.float32),
            jax.ShapeDtypeStruct((nblk, BLOCK, width), jnp.bfloat16),
        ],
        compiler_params=pltpu.CompilerParams(vmem_limit_bytes=VMEM_LIMIT),
        cost_estimate=pl.CostEstimate(
            flops=20_000_000_000, bytes_accessed=8_000_000, transcendentals=6_000_000
        ),
        name="index_back",
    )(picks, own, iq, wt, gathered, logits, target)


def tile_lists(picks):
    nblk = 64
    block = jnp.maximum(picks[:, 2:], 0).reshape(-1)
    npairs = block.shape[0]
    ntiles = -(-(npairs // PAIRS + nblk) // 2) * 2
    hot = (block[:, None] == jnp.arange(nblk)[None, :]).astype(jnp.int32)
    order = jnp.arange(npairs)
    same = (block[:, None] == block[None, :]) & (order[:, None] > order[None, :])
    rank = jnp.sum(same.astype(jnp.int32), axis=1)
    count = jnp.sum(hot, axis=0)
    padded = (count + PAIRS - 1) // PAIRS * PAIRS
    b = jnp.arange(nblk)
    start = jnp.sum(jnp.where(b[None, :] < b[:, None], padded[None, :], 0), axis=1)
    place = jnp.sum(hot * start[None, :], axis=1) + rank
    slots = jnp.arange(ntiles * PAIRS)
    found = place[None, :] == slots[:, None]
    pairs = jnp.sum(jnp.where(found, order[None, :] - npairs, 0), axis=1) + npairs
    ends = start + padded
    tile = jnp.arange(ntiles) * PAIRS
    owner = jnp.sum((ends[None, :] <= tile[:, None]).astype(jnp.int32), axis=1)
    owner = jnp.minimum(owner, nblk - 1)
    steps = (jnp.sum(padded) // PAIRS + 1) // 2
    tiles = jnp.concatenate([steps.reshape(1), owner])
    return tiles.astype(jnp.int32), pairs.astype(jnp.int32)


def axis_groups(stride):
    return [[b + k * stride for k in range(4)] for b in range(64) if (b // stride) % 4 == 0]


def swap_heads(x):
    return lax.ppermute(x, "head", [(0, 1), (1, 0)])


def head_sum(x):
    return x + swap_heads(x)


def join_halves(x, core):
    other = swap_heads(x)
    first = jnp.where(core == 0, x, other)
    second = jnp.where(core == 0, other, x)
    return jnp.concatenate([first, second], axis=0)


def pack_half(x):
    full = x.shape[1] // LANES
    tiles = x[:, : full * LANES].reshape(HALF, full, LANES).transpose(1, 0, 2).reshape(-1, LANES)
    last = x[:, full * LANES :]
    return jnp.concatenate([tiles, jnp.concatenate([last[: HALF // 2], last[HALF // 2 :]], axis=1)], axis=0)


def unpack_half(x):
    full = x.shape[0] // HALF
    tiles = x[: full * HALF].reshape(full, HALF, LANES).transpose(1, 0, 2).reshape(HALF, -1)
    last = x[full * HALF :]
    last = jnp.concatenate([last[:, :HALF], last[:, HALF:]], axis=0)
    return jnp.concatenate([tiles, last], axis=1)


def per_device(queries, latent, d_out, index_q, index_w, index_k, picks):
    rows, heads, width = queries.shape
    vwidth = d_out.shape[2]
    iheads, iwidth = index_q.shape[1:]
    wide = -(-width // LANES) * LANES
    core = lax.axis_index("head").astype(jnp.int32)
    own = jnp.stack([lax.axis_index("seq").astype(jnp.int32), core])
    picks_flat = picks.reshape(-1)

    lat_half = lax.dynamic_slice_in_dim(latent, core * HALF, HALF, 0)
    ik_half = lax.dynamic_slice_in_dim(index_k, core * HALF, HALF, 0)
    mine = jnp.concatenate([ik_half, pack_half(lat_half)], axis=0)
    gathered = lax.all_gather(mine, ("seq", "head"), axis=0, tiled=False)

    tiles, pairs = tile_lists(picks)
    stk = jnp.concatenate(
        [
            jnp.pad(queries, ((0, 0), (0, 0), (0, wide - width))),
            jnp.pad(d_out, ((0, 0), (0, 0), (0, wide - vwidth))),
        ],
        axis=1,
    )
    dsx, dsh, target_part, keep, send = attend_call(picks_flat, own, tiles, pairs, stk, gathered, heads)
    lat_sum = keep + swap_heads(send)
    for stride in (16, 4, 1):
        lat_sum = lax.psum_scatter(
            lat_sum, "seq", scatter_dimension=0, tiled=True, axis_index_groups=axis_groups(stride)
        )
    iq = index_q.reshape(rows * iheads, iwidth)
    wt = index_w.astype(jnp.float32).T
    logits = head_sum(index_logits_call(picks_flat, own, iq, wt, gathered, iheads, rows))
    target = head_sum(target_part)
    diq, dwt, dik = index_back_call(
        picks_flat, own, iq, wt, gathered, logits, target, iheads, rows
    )
    dik = dik.reshape(-1, 2, HALF, iwidth)
    ik_keep = lax.dynamic_index_in_dim(dik, core, 1, keepdims=False)
    ik_send = lax.dynamic_index_in_dim(dik, 1 - core, 1, keepdims=False)
    ik_sum = ik_keep + swap_heads(ik_send)
    ik_sum = lax.all_to_all(ik_sum, "seq", 0, 0, tiled=True)
    ik_sum = jnp.sum(ik_sum.astype(jnp.float32), axis=0).astype(jnp.bfloat16)
    dq = query_grad_call(own, tiles, pairs, dsx, dsh, gathered, heads, wide)

    d_latent = join_halves(unpack_half(lat_sum[0]), core)
    d_index_k = join_halves(ik_sum, core)
    d_queries = dq.reshape(rows, heads, wide)[:, :, :width]
    return (d_queries, d_latent, diq.reshape(rows, iheads, iwidth), dwt.T, d_index_k)


def solution(mesh):
    return jax.shard_map(
        per_device,
        mesh=mesh,
        in_specs=(
            P("seq", "head", None),
            P("seq", None),
            P("seq", "head", None),
            P("seq", "head", None),
            P("seq", "head"),
            P("seq", None),
            P("seq", None),
        ),
        out_specs=(
            P("seq", "head", None),
            P("seq", None),
            P("seq", "head", None),
            P("seq", "head"),
            P("seq", None),
        ),
        check_vma=False,
    )
```

```python
import functools

import jax
import jax.numpy as jnp
from jax import lax
from jax.experimental import pallas as pl
from jax.experimental.pallas import tpu as pltpu
from jax.sharding import PartitionSpec as P

BLOCK = 128
PICK = 4
H = 80
IH = 64
LANES = 128

softmax_scale = 192.0 ** (-0.5)
kl_weight = 32.0
neg_large = -1e30
inv_root = IH ** (-0.5)

G_ATT = 8
G_IDX = 8
UNROLL = 4
PAIRS = 4
HALF = BLOCK // 2
VMEM_LIMIT = 58 * 1024 * 1024


def dot(a, b, ca, cb):
    return lax.dot_general(a, b, (((ca,), (cb,)), ((), ())), preferred_element_type=jnp.float32)


def mask_row(picks_ref, t, tloc):
    lane = lax.broadcasted_iota(jnp.int32, (1, LANES), 1)
    parts = [jnp.where(lane <= tloc, 0.0, neg_large)]
    for j in range(1, PICK):
        parts.append(jnp.where(lane + picks_ref[t * PICK + j] * LANES >= 0, 0.0, neg_large))
    return jnp.concatenate(parts, axis=1)


def block_of(keys, b):
    return keys[pl.ds(2 * b, 2)].reshape(BLOCK, keys.shape[2])


def load_keys(lat_ref, keys, tails, sem):
    full = keys.shape[2] // LANES - 1
    copies = [
        pltpu.make_async_copy(
            lat_ref.at[:, pl.ds(c * HALF, HALF), :],
            keys.at[:, :, pl.ds(c * LANES, LANES)],
            sem.at[c],
        )
        for c in range(full)
    ]
    copies.append(
        pltpu.make_async_copy(
            lat_ref.at[:, pl.ds(full * HALF, HALF // 2), :], tails, sem.at[full]
        )
    )
    for cp in copies:
        cp.start()

    def finish():
        for cp in copies:
            cp.wait()

        def unpack(i, carry):
            low = tails[i]
            high = pltpu.roll(low.astype(jnp.float32), HALF, 1).astype(jnp.bfloat16)
            keys[i, :, pl.ds(full * LANES, LANES)] = jnp.concatenate([low, high], axis=0)
            return carry

        lax.fori_loop(0, keys.shape[0], unpack, 0, unroll=8)

    return finish


def attend_kernel(
    groups, heads, picks_ref, own_ref, tile_ref, pair_ref, stk_hbm, lat_ref,
    dsx_ref, dsh_ref, tgt_ref, keep_ref, send_ref,
    keys, tails, stk, extra, acc, acc_sh, sem,
):
    step = pl.program_id(0)
    own = own_ref[0]
    core = own_ref[1]
    rows = 2 * heads
    nblk = acc.shape[0]
    tokens = stk.shape[0]
    full = keys.shape[2] // LANES - 1

    @pl.when(step == 0)
    def _():
        chunk = tokens // full
        load_stk = [
            pltpu.make_async_copy(
                stk_hbm.at[pl.ds(c * chunk, chunk)], stk.at[pl.ds(c * chunk, chunk)], sem.at[full + 1 + c]
            )
            for c in range(full)
        ]
        finish = load_keys(lat_ref, keys, tails, sem)
        for cp in load_stk:
            cp.start()

        def zero(b, carry):
            acc[b] = jnp.zeros(acc.shape[1:], jnp.float32)
            return carry

        lax.fori_loop(0, nblk, zero, 0)
        acc_sh[...] = jnp.zeros(acc_sh.shape, jnp.float32)
        finish()
        for cp in load_stk:
            cp.wait()

        def tile_pair(i, carry):
            for u in range(UNROLL):
                tile = UNROLL * i + u
                pairs = [pair_ref[tile * PAIRS + k] for k in range(PAIRS)]
                lhs = jnp.concatenate([stk[jnp.minimum(p // 2, tokens - 1)] for p in pairs], axis=0)
                out = dot(lhs, block_of(keys, tile_ref[1 + tile]), 1, 1)
                for k, p in enumerate(pairs):
                    extra[p] = out[k * rows : (k + 1) * rows]
            return carry

        lax.fori_loop(0, tile_ref[0], tile_pair, 0)

    ksh = jnp.concatenate([block_of(keys, own), block_of(keys, 0)], axis=0)
    stk_all = stk[pl.ds(step * groups, groups)].reshape(groups * rows, stk.shape[2])
    both_sh = dot(stk_all, ksh, 1, 1)
    ds_list, gr_list, tgt_list = [], [], []
    for g in range(groups):
        t = step * groups + g
        e0 = jnp.maximum(picks_ref[t * PICK + 2], 0)
        e1 = jnp.maximum(picks_ref[t * PICK + 3], 0)
        bias = mask_row(picks_ref, t, t)
        both_x = jnp.concatenate([extra[2 * t], extra[2 * t + 1]], axis=1)
        lo = g * rows
        scores = jnp.concatenate([both_sh[lo : lo + heads], both_x[:heads]], axis=1)
        dprob = jnp.concatenate([both_sh[lo + heads : lo + rows], both_x[heads:]], axis=1)
        scores = scores * softmax_scale + bias
        top = jnp.max(scores, axis=1, keepdims=True)
        expo = jnp.exp(scores - top)
        probs = expo * (1.0 / jnp.sum(expo, axis=1, keepdims=True))
        delta = jnp.sum(probs * dprob, axis=1, keepdims=True)
        dscore = probs * (dprob - delta) * softmax_scale
        tgt_list.append(jnp.sum(probs, axis=0, keepdims=True))
        grads = jnp.concatenate([dscore, probs], axis=0).astype(jnp.bfloat16)
        dsx_ref[2 * g] = dscore[:, 2 * BLOCK : 3 * BLOCK]
        dsx_ref[2 * g + 1] = dscore[:, 3 * BLOCK :]
        upd = dot(grads[:, 2 * BLOCK :], stk[t], 0, 0)
        acc[e0] += upd[:BLOCK]
        acc[e1] += upd[BLOCK:]
        ds_list.append(dscore[:, : 2 * BLOCK])
        gr_list.append(grads[:, : 2 * BLOCK])
    dsh_ref[...] = jnp.concatenate(ds_list, axis=0).astype(jnp.bfloat16)
    acc_sh[...] += dot(jnp.concatenate(gr_list, axis=0), stk_all, 0, 0)
    tgt_ref[...] = jnp.concatenate(tgt_list, axis=0)

    @pl.when(step == pl.num_programs(0) - 1)
    def _():
        acc[own] += acc_sh[pl.ds(0, BLOCK), :]
        acc[0] += acc_sh[pl.ds(BLOCK, BLOCK), :]

        stores = []
        for k, ref, which in ((0, send_ref, 1 - core), (1, keep_ref, core)):
            rows_of = pl.ds(pl.multiple_of(which * HALF, HALF), HALF)
            part = pl.ds(k * nblk, nblk)

            def cast(b, carry):
                half = acc[b, rows_of, :]
                keys[k * nblk + b] = half.astype(jnp.bfloat16)
                last = half[:, full * LANES :]
                packed = last[: HALF // 2] + pltpu.roll(last[HALF // 2 :], HALF, 1)
                tails[k * nblk + b] = packed.astype(jnp.bfloat16)
                return carry

            lax.fori_loop(0, nblk, cast, 0, unroll=4)
            sent = [
                pltpu.make_async_copy(
                    keys.at[part, :, pl.ds(c * LANES, LANES)],
                    ref.at[:, pl.ds(c * HALF, HALF), :],
                    sem.at[k * (full + 1) + c],
                )
                for c in range(full)
            ]
            sent.append(
                pltpu.make_async_copy(
                    tails.at[part],
                    ref.at[:, pl.ds(full * HALF, HALF // 2), :],
                    sem.at[k * (full + 1) + full],
                )
            )
            for cp in sent:
                cp.start()
            stores += sent
        for cp in stores:
            cp.wait()


def attend_call(picks, own, tiles, pairs, stk, gathered, heads):
    tokens, rows, width = stk.shape
    nblk = gathered.shape[0] // 2
    full = width // LANES - 1
    groups = G_ATT
    packed = full * HALF + HALF // 2
    return pl.pallas_call(
        functools.partial(attend_kernel, groups, heads),
        grid_spec=pltpu.PrefetchScalarGridSpec(
            num_scalar_prefetch=4,
            grid=(tokens // groups,),
            in_specs=[pl.BlockSpec(memory_space=pl.ANY)] * 2,
            out_specs=[
                pl.BlockSpec((2 * groups, heads, BLOCK), lambda i, *_: (i, 0, 0)),
                pl.BlockSpec((groups * heads, 2 * BLOCK), lambda i, *_: (i, 0)),
                pl.BlockSpec((groups, PICK * BLOCK), lambda i, *_: (i, 0)),
                pl.BlockSpec(memory_space=pl.ANY),
                pl.BlockSpec(memory_space=pl.ANY),
            ],
            scratch_shapes=[
                pltpu.VMEM((2 * nblk, HALF, width), jnp.bfloat16),
                pltpu.VMEM((2 * nblk, HALF // 2, LANES), jnp.bfloat16),
                pltpu.VMEM((tokens, rows, width), jnp.bfloat16),
                pltpu.VMEM((2 * tokens + 1, rows, BLOCK), jnp.float32),
                pltpu.VMEM((nblk, BLOCK, width), jnp.float32),
                pltpu.VMEM((2 * BLOCK, width), jnp.float32),
                pltpu.SemaphoreType.DMA((2 * full + 2,)),
            ],
        ),
        out_shape=[
            jax.ShapeDtypeStruct((2 * tokens, heads, BLOCK), jnp.float32),
            jax.ShapeDtypeStruct((tokens * heads, 2 * BLOCK), jnp.bfloat16),
            jax.ShapeDtypeStruct((tokens, PICK * BLOCK), jnp.float32),
            jax.ShapeDtypeStruct((nblk, packed, LANES), jnp.bfloat16),
            jax.ShapeDtypeStruct((nblk, packed, LANES), jnp.bfloat16),
        ],
        compiler_params=pltpu.CompilerParams(vmem_limit_bytes=VMEM_LIMIT),
        cost_estimate=pl.CostEstimate(
            flops=60_000_000_000, bytes_accessed=50_000_000, transcendentals=3_000_000
        ),
        name="attend",
    )(picks, own, tiles, pairs, stk, gathered)


def query_grad_kernel(groups, heads, own_ref, tile_ref, pair_ref, dsx_ref, dsh_ref, lat_ref, dq_ref, keys, tails, total, sem):
    own = own_ref[0]
    npairs = dsx_ref.shape[0]
    width = keys.shape[2]
    finish = load_keys(lat_ref, keys, tails, sem)

    def zero(t, carry):
        total[t] = jnp.zeros(total.shape[1:], jnp.float32)
        return carry

    lax.fori_loop(0, total.shape[0], zero, 0)
    finish()

    def tile_pair(i, carry):
        for u in range(UNROLL):
            tile = UNROLL * i + u
            pairs = [pair_ref[tile * PAIRS + k] for k in range(PAIRS)]
            lhs = jnp.concatenate([dsx_ref[jnp.minimum(p, npairs - 1)] for p in pairs], axis=0)
            out = dot(lhs.astype(jnp.bfloat16), block_of(keys, tile_ref[1 + tile]), 1, 0)
            for k, p in enumerate(pairs):
                total[p // 2] += out[k * heads : (k + 1) * heads]
        return carry

    lax.fori_loop(0, tile_ref[0], tile_pair, 0)
    ksh = jnp.concatenate([block_of(keys, own), block_of(keys, 0)], axis=0)

    def shared(i, carry):
        part = pl.ds(pl.multiple_of(i * groups * heads, groups * heads), groups * heads)
        out = dot(dsh_ref[part, :], ksh, 1, 0)
        out = out + total[pl.ds(i * groups, groups)].reshape(groups * heads, width)
        dq_ref[part, :] = out.astype(jnp.bfloat16)
        return carry

    lax.fori_loop(0, dsh_ref.shape[0] // (groups * heads), shared, 0)


def query_grad_call(own, tiles, pairs, dsx, dsh, gathered, heads, width):
    tokens = dsx.shape[0] // 2
    nblk = gathered.shape[0] // 2
    full = width // LANES - 1
    vmem = pl.BlockSpec(memory_space=pltpu.VMEM)
    smem = pl.BlockSpec(memory_space=pltpu.SMEM)
    return pl.pallas_call(
        functools.partial(query_grad_kernel, 8, heads),
        in_specs=[smem, smem, smem, vmem, vmem, pl.BlockSpec(memory_space=pl.ANY)],
        out_specs=vmem,
        out_shape=jax.ShapeDtypeStruct((tokens * heads, width), jnp.bfloat16),
        scratch_shapes=[
            pltpu.VMEM((2 * nblk, HALF, width), jnp.bfloat16),
            pltpu.VMEM((2 * nblk, HALF // 2, LANES), jnp.bfloat16),
            pltpu.VMEM((tokens + 1, heads, width), jnp.float32),
            pltpu.SemaphoreType.DMA((full + 1,)),
        ],
        compiler_params=pltpu.CompilerParams(vmem_limit_bytes=VMEM_LIMIT),
        cost_estimate=pl.CostEstimate(
            flops=12_000_000_000, bytes_accessed=25_000_000, transcendentals=0
        ),
        name="query_grad",
    )(own, tiles, pairs, dsx, dsh, gathered)


def softplus(x):
    return jnp.maximum(x, 0.0) + jnp.log(1.0 + jnp.exp(-jnp.abs(x)))


def weight_column(wt, t):
    lane = lax.broadcasted_iota(jnp.int32, wt.shape, 1)
    return jnp.sum(jnp.where(lane == t, wt, 0.0), axis=1, keepdims=True)


def index_logits_kernel(groups, heads, picks_ref, own_ref, iq_ref, wt_ref, ik_ref, gate_ref, out_ref):
    step = pl.program_id(0)
    own = own_ref[0]
    ksh = jnp.concatenate([block_of(ik_ref, own), block_of(ik_ref, 0)], axis=0)
    gate_sh = dot(iq_ref[...], ksh, 1, 1)
    wt = wt_ref[...]
    outs = []
    for g in range(groups):
        t = step * groups + g
        e0 = jnp.maximum(picks_ref[t * PICK + 2], 0)
        e1 = jnp.maximum(picks_ref[t * PICK + 3], 0)
        kx = jnp.concatenate([block_of(ik_ref, e0), block_of(ik_ref, e1)], axis=0)
        gate_x = dot(iq_ref[pl.ds(g * heads, heads), :], kx, 1, 1)
        gate = jnp.concatenate([gate_sh[g * heads : (g + 1) * heads], gate_x], axis=1)
        gate_ref[pl.ds(g * heads, heads), :] = gate
        w = weight_column(wt, t)
        outs.append(jnp.sum(w * softplus(gate), axis=0, keepdims=True))
    out_ref[...] = jnp.concatenate(outs, axis=0) * inv_root


def index_back_kernel(
    groups, heads, picks_ref, own_ref, iq_ref, wt_ref, ik_ref, gate_ref, logit_ref, tgt_ref, diq_ref, dwt_ref, dik_ref, acc, acc_sh
):
    step = pl.program_id(0)
    own = own_ref[0]

    @pl.when(step == 0)
    def _():
        acc[...] = jnp.zeros(acc.shape, jnp.float32)
        acc_sh[...] = jnp.zeros(acc_sh.shape, jnp.float32)
        dwt_ref[...] = jnp.zeros(dwt_ref.shape, jnp.float32)

    bias = jnp.concatenate(
        [mask_row(picks_ref, step * groups + g, step * groups + g) for g in range(groups)], axis=0
    )
    logits = logit_ref[...] + bias
    top = jnp.max(logits, axis=1, keepdims=True)
    expo = jnp.exp(logits - top)
    soft = expo * (1.0 / jnp.sum(expo, axis=1, keepdims=True))
    d_logit_all = jnp.where(bias == 0.0, kl_weight * (soft - tgt_ref[...] * (1.0 / H)), 0.0)

    ksh = jnp.concatenate([block_of(ik_ref, own), block_of(ik_ref, 0)], axis=0)
    wt = wt_ref[...]
    lane = lax.broadcasted_iota(jnp.int32, wt.shape, 1)
    dwt = dwt_ref[...]
    dg_list, dx_list = [], []
    for g in range(groups):
        t = step * groups + g
        e0 = jnp.maximum(picks_ref[t * PICK + 2], 0)
        e1 = jnp.maximum(picks_ref[t * PICK + 3], 0)
        kx = jnp.concatenate([block_of(ik_ref, e0), block_of(ik_ref, e1)], axis=0)
        iq_g = iq_ref[pl.ds(g * heads, heads), :]
        gate = gate_ref[pl.ds(g * heads, heads), :]
        w = weight_column(wt, t)
        d_logit = d_logit_all[g : g + 1]
        small = jnp.exp(-jnp.abs(gate))
        denom = 1.0 + small
        soft_gate = jnp.maximum(gate, 0.0) + jnp.log(denom)
        sig = jnp.where(gate >= 0.0, 1.0, small) / denom
        dw = jnp.sum(d_logit * soft_gate, axis=1, keepdims=True) * inv_root
        dwt = jnp.where(lane == t, dw, dwt)
        d_gate = (d_logit * (w * inv_root) * sig).astype(jnp.bfloat16)
        gx = d_gate[:, 2 * BLOCK :]
        dx_list.append(dot(gx, kx, 1, 0))
        upd = dot(gx, iq_g, 0, 0)
        acc[e0] += upd[:BLOCK]
        acc[e1] += upd[BLOCK:]
        dg_list.append(d_gate[:, : 2 * BLOCK])
    dwt_ref[...] = dwt
    dg_sh = jnp.concatenate(dg_list, axis=0)
    diq = dot(dg_sh, ksh, 1, 0) + jnp.concatenate(dx_list, axis=0)
    diq_ref[...] = diq.astype(jnp.bfloat16)
    acc_sh[...] += dot(dg_sh, iq_ref[...], 0, 0)

    @pl.when(step == pl.num_programs(0) - 1)
    def _():
        acc[own] += acc_sh[pl.ds(0, BLOCK), :]
        acc[0] += acc_sh[pl.ds(BLOCK, BLOCK), :]
        dik_ref[...] = acc[...].astype(jnp.bfloat16)


def index_logits_call(picks, own, iq, wt, gathered, heads, tokens):
    groups = G_IDX
    span = PICK * BLOCK
    return pl.pallas_call(
        functools.partial(index_logits_kernel, groups, heads),
        grid_spec=pltpu.PrefetchScalarGridSpec(
            num_scalar_prefetch=2,
            grid=(tokens // groups,),
            in_specs=[
                pl.BlockSpec((groups * heads, iq.shape[1]), lambda i, *_: (i, 0)),
                pl.BlockSpec(wt.shape, lambda i, *_: (0, 0)),
                pl.BlockSpec((gathered.shape[0], HALF, LANES), lambda i, *_: (0, 0, 0)),
            ],
            out_specs=[
                pl.BlockSpec((groups * heads, span), lambda i, *_: (i, 0)),
                pl.BlockSpec((groups, span), lambda i, *_: (i, 0)),
            ],
        ),
        out_shape=[
            jax.ShapeDtypeStruct((tokens * heads, span), jnp.float32),
            jax.ShapeDtypeStruct((tokens, span), jnp.float32),
        ],
        compiler_params=pltpu.CompilerParams(vmem_limit_bytes=VMEM_LIMIT),
        cost_estimate=pl.CostEstimate(
            flops=10_000_000_000, bytes_accessed=4_000_000, transcendentals=6_000_000
        ),
        name="index_logits",
    )(picks, own, iq, wt, gathered)


def index_back_call(picks, own, iq, wt, gathered, gate, logits, target, heads, tokens):
    groups = G_IDX
    span = PICK * BLOCK
    width = iq.shape[1]
    nblk = gathered.shape[0] // 2
    return pl.pallas_call(
        functools.partial(index_back_kernel, groups, heads),
        grid_spec=pltpu.PrefetchScalarGridSpec(
            num_scalar_prefetch=2,
            grid=(tokens // groups,),
            in_specs=[
                pl.BlockSpec((groups * heads, width), lambda i, *_: (i, 0)),
                pl.BlockSpec(wt.shape, lambda i, *_: (0, 0)),
                pl.BlockSpec((gathered.shape[0], HALF, LANES), lambda i, *_: (0, 0, 0)),
                pl.BlockSpec((groups * heads, span), lambda i, *_: (i, 0)),
                pl.BlockSpec((groups, span), lambda i, *_: (i, 0)),
                pl.BlockSpec((groups, span), lambda i, *_: (i, 0)),
            ],
            out_specs=[
                pl.BlockSpec((groups * heads, width), lambda i, *_: (i, 0)),
                pl.BlockSpec((heads, tokens), lambda i, *_: (0, 0)),
                pl.BlockSpec((nblk, BLOCK, width), lambda i, *_: (0, 0, 0)),
            ],
            scratch_shapes=[
                pltpu.VMEM((nblk, BLOCK, width), jnp.float32),
                pltpu.VMEM((2 * BLOCK, width), jnp.float32),
            ],
        ),
        out_shape=[
            jax.ShapeDtypeStruct((tokens * heads, width), jnp.bfloat16),
            jax.ShapeDtypeStruct((heads, tokens), jnp.float32),
            jax.ShapeDtypeStruct((nblk, BLOCK, width), jnp.bfloat16),
        ],
        compiler_params=pltpu.CompilerParams(vmem_limit_bytes=VMEM_LIMIT),
        cost_estimate=pl.CostEstimate(
            flops=20_000_000_000, bytes_accessed=8_000_000, transcendentals=6_000_000
        ),
        name="index_back",
    )(picks, own, iq, wt, gathered, gate, logits, target)


def tile_lists(picks):
    nblk = 64
    block = jnp.maximum(picks[:, 2:], 0).reshape(-1)
    npairs = block.shape[0]
    ntiles = -(-(npairs // PAIRS + nblk) // UNROLL) * UNROLL
    hot = (block[:, None] == jnp.arange(nblk)[None, :]).astype(jnp.int32)
    order = jnp.arange(npairs)
    same = (block[:, None] == block[None, :]) & (order[:, None] > order[None, :])
    rank = jnp.sum(same.astype(jnp.int32), axis=1)
    count = jnp.sum(hot, axis=0)
    padded = (count + PAIRS - 1) // PAIRS * PAIRS
    b = jnp.arange(nblk)
    start = jnp.sum(jnp.where(b[None, :] < b[:, None], padded[None, :], 0), axis=1)
    place = jnp.sum(hot * start[None, :], axis=1) + rank
    slots = jnp.arange(ntiles * PAIRS)
    found = place[None, :] == slots[:, None]
    pairs = jnp.sum(jnp.where(found, order[None, :] - npairs, 0), axis=1) + npairs
    ends = start + padded
    tile = jnp.arange(ntiles) * PAIRS
    owner = jnp.sum((ends[None, :] <= tile[:, None]).astype(jnp.int32), axis=1)
    owner = jnp.minimum(owner, nblk - 1)
    steps = (jnp.sum(padded) // PAIRS + UNROLL - 1) // UNROLL
    tiles = jnp.concatenate([steps.reshape(1), owner])
    return tiles.astype(jnp.int32), pairs.astype(jnp.int32)


def swap_heads(x):
    return lax.ppermute(x, "head", [(0, 1), (1, 0)])


def head_sum(x):
    return x + swap_heads(x)


def add_parts(parts):
    return jnp.sum(parts.astype(jnp.float32), axis=0).astype(parts.dtype)


def gather_by_exchange(x, core):
    mine = lax.all_to_all(jnp.broadcast_to(x[None], (64,) + x.shape), "seq", 0, 0, tiled=True)
    other = swap_heads(mine)
    first = jnp.where(core == 0, mine, other)
    second = jnp.where(core == 0, other, mine)
    return jnp.stack([first, second], axis=1).reshape((-1,) + x.shape)


def join_halves(x, core):
    other = swap_heads(x)
    first = jnp.where(core == 0, x, other)
    second = jnp.where(core == 0, other, x)
    return jnp.concatenate([first, second], axis=0)


def pack_half(x):
    full = x.shape[1] // LANES
    tiles = x[:, : full * LANES].reshape(HALF, full, LANES).transpose(1, 0, 2).reshape(-1, LANES)
    last = x[:, full * LANES :]
    return jnp.concatenate([tiles, jnp.concatenate([last[: HALF // 2], last[HALF // 2 :]], axis=1)], axis=0)


def unpack_half(x):
    full = x.shape[0] // HALF
    tiles = x[: full * HALF].reshape(full, HALF, LANES).transpose(1, 0, 2).reshape(HALF, -1)
    last = x[full * HALF :]
    last = jnp.concatenate([last[:, :HALF], last[:, HALF:]], axis=0)
    return jnp.concatenate([tiles, last], axis=1)


def per_device(queries, latent, d_out, index_q, index_w, index_k, picks):
    rows, heads, width = queries.shape
    vwidth = d_out.shape[2]
    iheads, iwidth = index_q.shape[1:]
    wide = -(-width // LANES) * LANES
    core = lax.axis_index("head").astype(jnp.int32)
    own = jnp.stack([lax.axis_index("seq").astype(jnp.int32), core])
    picks_flat = picks.reshape(-1)

    lat_half = lax.dynamic_slice_in_dim(latent, core * HALF, HALF, 0)
    ik_half = lax.dynamic_slice_in_dim(index_k, core * HALF, HALF, 0)
    gathered = lax.all_gather(pack_half(lat_half), ("seq", "head"), axis=0, tiled=False)
    ik_all = gather_by_exchange(ik_half, core)

    iq = index_q.reshape(rows * iheads, iwidth)
    wt = index_w.astype(jnp.float32).T
    gate, logit_part = index_logits_call(picks_flat, own, iq, wt, ik_all, iheads, rows)

    tiles, pairs = tile_lists(picks)
    stk = jnp.concatenate(
        [
            jnp.pad(queries, ((0, 0), (0, 0), (0, wide - width))),
            jnp.pad(d_out, ((0, 0), (0, 0), (0, wide - vwidth))),
        ],
        axis=1,
    )
    own_next, logit_part = lax.optimization_barrier((own, logit_part))
    dsx, dsh, target_part, keep, send = attend_call(picks_flat, own_next, tiles, pairs, stk, gathered, heads)
    lat_part = keep + swap_heads(send)
    target_part, lat_part = lax.optimization_barrier((target_part, lat_part))
    lat_parts = lax.all_to_all(lat_part, "seq", 0, 0, tiled=True)
    target = head_sum(target_part)
    logits = head_sum(logit_part)
    diq, dwt, dik = index_back_call(
        picks_flat, own, iq, wt, ik_all, gate, logits, target, iheads, rows
    )
    dik = dik.reshape(-1, 2, HALF, iwidth)
    ik_keep = lax.dynamic_index_in_dim(dik, core, 1, keepdims=False)
    ik_send = lax.dynamic_index_in_dim(dik, 1 - core, 1, keepdims=False)
    ik_part = ik_keep + swap_heads(ik_send)
    own_late, ik_part = lax.optimization_barrier((own, ik_part))
    dq = query_grad_call(own_late, tiles, pairs, dsx, dsh, gathered, heads, wide)
    dq = dq.reshape(rows, heads, wide)[:, :, :width].transpose(1, 2, 0)
    dq, ik_part, lat_parts = lax.optimization_barrier((dq, ik_part, lat_parts))
    ik_parts = lax.all_to_all(ik_part, "seq", 0, 0, tiled=True)
    lat_sum = add_parts(lat_parts)
    ik_sum = add_parts(ik_parts)

    d_latent = join_halves(unpack_half(lat_sum), core)
    d_index_k = join_halves(ik_sum, core)
    d_queries = dq.transpose(2, 0, 1)
    return (d_queries, d_latent, diq.reshape(rows, iheads, iwidth), dwt.T, d_index_k)


def solution(mesh):
    return jax.shard_map(
        per_device,
        mesh=mesh,
        in_specs=(
            P("seq", "head", None),
            P("seq", None),
            P("seq", "head", None),
            P("seq", "head", None),
            P("seq", "head"),
            P("seq", None),
            P("seq", None),
        ),
        out_specs=(
            P("seq", "head", None),
            P("seq", None),
            P("seq", "head", None),
            P("seq", "head"),
            P("seq", None),
        ),
        check_vma=False,
    )
```

```python
import functools

import jax
import jax.numpy as jnp
from jax import lax
from jax.experimental import pallas as pl
from jax.experimental.pallas import tpu as pltpu
from jax.sharding import PartitionSpec as P

BLOCK = 128
PICK = 4
H = 80
IH = 64
LANES = 128

softmax_scale = 192.0 ** (-0.5)
kl_weight = 32.0
neg_large = -1e30
inv_root = IH ** (-0.5)

G_ATT = 16
G_IDX = 8
UNROLL = 4
PAIRS = 4
HALF = BLOCK // 2
VMEM_LIMIT = 60 * 1024 * 1024


def dot(a, b, ca, cb):
    return lax.dot_general(a, b, (((ca,), (cb,)), ((), ())), preferred_element_type=jnp.float32)


def mask_row(picks_ref, t, tloc):
    lane = lax.broadcasted_iota(jnp.int32, (1, LANES), 1)
    parts = [jnp.where(lane <= tloc, 0.0, neg_large)]
    for j in range(1, PICK):
        parts.append(jnp.where(lane + picks_ref[t * PICK + j] * LANES >= 0, 0.0, neg_large))
    return jnp.concatenate(parts, axis=1)


def block_of(keys, b):
    return keys[pl.ds(2 * b, 2)].reshape(BLOCK, keys.shape[2])


def load_keys(lat_ref, keys, tails, sem):
    full = keys.shape[2] // LANES - 1
    copies = [
        pltpu.make_async_copy(
            lat_ref.at[:, pl.ds(c * HALF, HALF), :],
            keys.at[:, :, pl.ds(c * LANES, LANES)],
            sem.at[c],
        )
        for c in range(full)
    ]
    copies.append(
        pltpu.make_async_copy(
            lat_ref.at[:, pl.ds(full * HALF, HALF // 2), :], tails, sem.at[full]
        )
    )
    for cp in copies:
        cp.start()

    def finish():
        for cp in copies:
            cp.wait()

        def unpack(i, carry):
            low = tails[i]
            high = pltpu.roll(low.astype(jnp.float32), HALF, 1).astype(jnp.bfloat16)
            keys[i, :, pl.ds(full * LANES, LANES)] = jnp.concatenate([low, high], axis=0)
            return carry

        lax.fori_loop(0, keys.shape[0], unpack, 0, unroll=8)

    return finish


def attend_kernel(
    groups, heads, picks_ref, own_ref, tile_ref, pair_ref, stk_hbm, lat_ref,
    dsx_ref, dsh_ref, tgt_ref, keep_ref, send_ref,
    keys, tails, stk, extra, acc, acc_sh, sem,
):
    step = pl.program_id(0)
    own = own_ref[0]
    core = own_ref[1]
    rows = 2 * heads
    nblk = acc.shape[0]
    tokens = stk.shape[0]
    full = keys.shape[2] // LANES - 1

    @pl.when(step == 0)
    def _():
        chunk = tokens // full
        load_stk = [
            pltpu.make_async_copy(
                stk_hbm.at[pl.ds(c * chunk, chunk)], stk.at[pl.ds(c * chunk, chunk)], sem.at[full + 1 + c]
            )
            for c in range(full)
        ]
        finish = load_keys(lat_ref, keys, tails, sem)
        for cp in load_stk:
            cp.start()

        def zero(b, carry):
            acc[b] = jnp.zeros(acc.shape[1:], jnp.float32)
            return carry

        lax.fori_loop(0, nblk, zero, 0)
        acc_sh[...] = jnp.zeros(acc_sh.shape, jnp.float32)
        finish()
        for cp in load_stk:
            cp.wait()

        def tile_pair(i, carry):
            for u in range(UNROLL):
                tile = UNROLL * i + u
                pairs = [pair_ref[tile * PAIRS + k] for k in range(PAIRS)]
                lhs = jnp.concatenate([stk[jnp.minimum(p // 2, tokens - 1)] for p in pairs], axis=0)
                out = dot(lhs, block_of(keys, tile_ref[1 + tile]), 1, 1)
                for k, p in enumerate(pairs):
                    extra[p] = out[k * rows : (k + 1) * rows]
            return carry

        lax.fori_loop(0, tile_ref[0], tile_pair, 0)

    ksh = jnp.concatenate([block_of(keys, own), block_of(keys, 0)], axis=0)
    stk_all = stk[pl.ds(step * groups, groups)].reshape(groups * rows, stk.shape[2])
    both_sh = dot(stk_all, ksh, 1, 1)
    ds_list, gr_list, tgt_list = [], [], []
    for g in range(groups):
        t = step * groups + g
        e0 = jnp.maximum(picks_ref[t * PICK + 2], 0)
        e1 = jnp.maximum(picks_ref[t * PICK + 3], 0)
        bias = mask_row(picks_ref, t, t)
        both_x = jnp.concatenate([extra[2 * t], extra[2 * t + 1]], axis=1)
        lo = g * rows
        scores = jnp.concatenate([both_sh[lo : lo + heads], both_x[:heads]], axis=1)
        dprob = jnp.concatenate([both_sh[lo + heads : lo + rows], both_x[heads:]], axis=1)
        scores = scores * softmax_scale + bias
        top = jnp.max(scores, axis=1, keepdims=True)
        expo = jnp.exp(scores - top)
        probs = expo * (1.0 / jnp.sum(expo, axis=1, keepdims=True))
        delta = jnp.sum(probs * dprob, axis=1, keepdims=True)
        dscore = probs * (dprob - delta) * softmax_scale
        tgt_list.append(jnp.sum(probs, axis=0, keepdims=True))
        grads = jnp.concatenate([dscore, probs], axis=0).astype(jnp.bfloat16)
        dsx_ref[2 * g] = dscore[:, 2 * BLOCK : 3 * BLOCK]
        dsx_ref[2 * g + 1] = dscore[:, 3 * BLOCK :]
        upd = dot(grads[:, 2 * BLOCK :], stk[t], 0, 0)
        acc[e0] += upd[:BLOCK]
        acc[e1] += upd[BLOCK:]
        ds_list.append(dscore[:, : 2 * BLOCK])
        gr_list.append(grads[:, : 2 * BLOCK])
    dsh_ref[...] = jnp.concatenate(ds_list, axis=0).astype(jnp.bfloat16)
    acc_sh[...] += dot(jnp.concatenate(gr_list, axis=0), stk_all, 0, 0)
    tgt_ref[...] = jnp.concatenate(tgt_list, axis=0)

    @pl.when(step == pl.num_programs(0) - 1)
    def _():
        acc[own] += acc_sh[pl.ds(0, BLOCK), :]
        acc[0] += acc_sh[pl.ds(BLOCK, BLOCK), :]

        stores = []
        for k, ref, which in ((0, send_ref, 1 - core), (1, keep_ref, core)):
            rows_of = pl.ds(pl.multiple_of(which * HALF, HALF), HALF)
            part = pl.ds(k * nblk, nblk)

            def cast(b, carry):
                half = acc[b, rows_of, :]
                keys[k * nblk + b] = half.astype(jnp.bfloat16)
                last = half[:, full * LANES :]
                packed = last[: HALF // 2] + pltpu.roll(last[HALF // 2 :], HALF, 1)
                tails[k * nblk + b] = packed.astype(jnp.bfloat16)
                return carry

            lax.fori_loop(0, nblk, cast, 0, unroll=4)
            sent = [
                pltpu.make_async_copy(
                    keys.at[part, :, pl.ds(c * LANES, LANES)],
                    ref.at[:, pl.ds(c * HALF, HALF), :],
                    sem.at[k * (full + 1) + c],
                )
                for c in range(full)
            ]
            sent.append(
                pltpu.make_async_copy(
                    tails.at[part],
                    ref.at[:, pl.ds(full * HALF, HALF // 2), :],
                    sem.at[k * (full + 1) + full],
                )
            )
            for cp in sent:
                cp.start()
            stores += sent
        for cp in stores:
            cp.wait()


def attend_call(picks, own, tiles, pairs, stk, gathered, heads):
    tokens, rows, width = stk.shape
    nblk = gathered.shape[0] // 2
    full = width // LANES - 1
    groups = G_ATT
    packed = full * HALF + HALF // 2
    return pl.pallas_call(
        functools.partial(attend_kernel, groups, heads),
        grid_spec=pltpu.PrefetchScalarGridSpec(
            num_scalar_prefetch=4,
            grid=(tokens // groups,),
            in_specs=[pl.BlockSpec(memory_space=pl.ANY)] * 2,
            out_specs=[
                pl.BlockSpec((2 * groups, heads, BLOCK), lambda i, *_: (i, 0, 0)),
                pl.BlockSpec((groups * heads, 2 * BLOCK), lambda i, *_: (i, 0)),
                pl.BlockSpec((groups, PICK * BLOCK), lambda i, *_: (i, 0)),
                pl.BlockSpec(memory_space=pl.ANY),
                pl.BlockSpec(memory_space=pl.ANY),
            ],
            scratch_shapes=[
                pltpu.VMEM((2 * nblk, HALF, width), jnp.bfloat16),
                pltpu.VMEM((2 * nblk, HALF // 2, LANES), jnp.bfloat16),
                pltpu.VMEM((tokens, rows, width), jnp.bfloat16),
                pltpu.VMEM((2 * tokens + 1, rows, BLOCK), jnp.float32),
                pltpu.VMEM((nblk, BLOCK, width), jnp.float32),
                pltpu.VMEM((2 * BLOCK, width), jnp.float32),
                pltpu.SemaphoreType.DMA((2 * full + 2,)),
            ],
        ),
        out_shape=[
            jax.ShapeDtypeStruct((2 * tokens, heads, BLOCK), jnp.float32),
            jax.ShapeDtypeStruct((tokens * heads, 2 * BLOCK), jnp.bfloat16),
            jax.ShapeDtypeStruct((tokens, PICK * BLOCK), jnp.float32),
            jax.ShapeDtypeStruct((nblk, packed, LANES), jnp.bfloat16),
            jax.ShapeDtypeStruct((nblk, packed, LANES), jnp.bfloat16),
        ],
        compiler_params=pltpu.CompilerParams(vmem_limit_bytes=VMEM_LIMIT),
        cost_estimate=pl.CostEstimate(
            flops=60_000_000_000, bytes_accessed=50_000_000, transcendentals=3_000_000
        ),
        name="attend",
    )(picks, own, tiles, pairs, stk, gathered)


def query_grad_kernel(groups, heads, own_ref, tile_ref, pair_ref, dsx_ref, dsh_ref, lat_ref, dq_ref, keys, tails, total, sem):
    own = own_ref[0]
    npairs = dsx_ref.shape[0]
    width = keys.shape[2]
    finish = load_keys(lat_ref, keys, tails, sem)

    def zero(t, carry):
        total[t] = jnp.zeros(total.shape[1:], jnp.float32)
        return carry

    lax.fori_loop(0, total.shape[0], zero, 0)
    finish()

    def tile_pair(i, carry):
        for u in range(UNROLL):
            tile = UNROLL * i + u
            pairs = [pair_ref[tile * PAIRS + k] for k in range(PAIRS)]
            lhs = jnp.concatenate([dsx_ref[jnp.minimum(p, npairs - 1)] for p in pairs], axis=0)
            out = dot(lhs.astype(jnp.bfloat16), block_of(keys, tile_ref[1 + tile]), 1, 0)
            for k, p in enumerate(pairs):
                total[p // 2] += out[k * heads : (k + 1) * heads]
        return carry

    lax.fori_loop(0, tile_ref[0], tile_pair, 0)
    ksh = jnp.concatenate([block_of(keys, own), block_of(keys, 0)], axis=0)

    def shared(i, carry):
        part = pl.ds(pl.multiple_of(i * groups * heads, groups * heads), groups * heads)
        out = dot(dsh_ref[part, :], ksh, 1, 0)
        out = out + total[pl.ds(i * groups, groups)].reshape(groups * heads, width)
        dq_ref[part, :] = out.astype(jnp.bfloat16)
        return carry

    lax.fori_loop(0, dsh_ref.shape[0] // (groups * heads), shared, 0)


def query_grad_call(own, tiles, pairs, dsx, dsh, gathered, heads, width):
    tokens = dsx.shape[0] // 2
    nblk = gathered.shape[0] // 2
    full = width // LANES - 1
    vmem = pl.BlockSpec(memory_space=pltpu.VMEM)
    smem = pl.BlockSpec(memory_space=pltpu.SMEM)
    return pl.pallas_call(
        functools.partial(query_grad_kernel, 8, heads),
        in_specs=[smem, smem, smem, vmem, vmem, pl.BlockSpec(memory_space=pl.ANY)],
        out_specs=vmem,
        out_shape=jax.ShapeDtypeStruct((tokens * heads, width), jnp.bfloat16),
        scratch_shapes=[
            pltpu.VMEM((2 * nblk, HALF, width), jnp.bfloat16),
            pltpu.VMEM((2 * nblk, HALF // 2, LANES), jnp.bfloat16),
            pltpu.VMEM((tokens + 1, heads, width), jnp.float32),
            pltpu.SemaphoreType.DMA((full + 1,)),
        ],
        compiler_params=pltpu.CompilerParams(vmem_limit_bytes=VMEM_LIMIT),
        cost_estimate=pl.CostEstimate(
            flops=12_000_000_000, bytes_accessed=25_000_000, transcendentals=0
        ),
        name="query_grad",
    )(own, tiles, pairs, dsx, dsh, gathered)


def softplus(x):
    return jnp.maximum(x, 0.0) + jnp.log(1.0 + jnp.exp(-jnp.abs(x)))


def weight_column(wt, t):
    lane = lax.broadcasted_iota(jnp.int32, wt.shape, 1)
    return jnp.sum(jnp.where(lane == t, wt, 0.0), axis=1, keepdims=True)


def index_logits_kernel(groups, heads, picks_ref, own_ref, iq_ref, wt_ref, ik_ref, gate_ref, out_ref):
    step = pl.program_id(0)
    own = own_ref[0]
    ksh = jnp.concatenate([block_of(ik_ref, own), block_of(ik_ref, 0)], axis=0)
    gate_sh = dot(iq_ref[...], ksh, 1, 1)
    wt = wt_ref[...]
    outs = []
    for g in range(groups):
        t = step * groups + g
        e0 = jnp.maximum(picks_ref[t * PICK + 2], 0)
        e1 = jnp.maximum(picks_ref[t * PICK + 3], 0)
        kx = jnp.concatenate([block_of(ik_ref, e0), block_of(ik_ref, e1)], axis=0)
        gate_x = dot(iq_ref[pl.ds(g * heads, heads), :], kx, 1, 1)
        gate = jnp.concatenate([gate_sh[g * heads : (g + 1) * heads], gate_x], axis=1)
        gate_ref[pl.ds(g * heads, heads), :] = gate
        w = weight_column(wt, t)
        outs.append(jnp.sum(w * softplus(gate), axis=0, keepdims=True))
    out_ref[...] = jnp.concatenate(outs, axis=0) * inv_root


def index_back_kernel(
    groups, heads, picks_ref, own_ref, iq_ref, wt_ref, ik_ref, gate_ref, logit_ref, tgt_ref, diq_ref, dwt_ref, dik_ref, acc, acc_sh
):
    step = pl.program_id(0)
    own = own_ref[0]

    @pl.when(step == 0)
    def _():
        acc[...] = jnp.zeros(acc.shape, jnp.float32)
        acc_sh[...] = jnp.zeros(acc_sh.shape, jnp.float32)
        dwt_ref[...] = jnp.zeros(dwt_ref.shape, jnp.float32)

    bias = jnp.concatenate(
        [mask_row(picks_ref, step * groups + g, step * groups + g) for g in range(groups)], axis=0
    )
    logits = logit_ref[...] + bias
    top = jnp.max(logits, axis=1, keepdims=True)
    expo = jnp.exp(logits - top)
    soft = expo * (1.0 / jnp.sum(expo, axis=1, keepdims=True))
    d_logit_all = jnp.where(bias == 0.0, kl_weight * (soft - tgt_ref[...] * (1.0 / H)), 0.0)

    ksh = jnp.concatenate([block_of(ik_ref, own), block_of(ik_ref, 0)], axis=0)
    wt = wt_ref[...]
    lane = lax.broadcasted_iota(jnp.int32, wt.shape, 1)
    dwt = dwt_ref[...]
    dg_list, dx_list = [], []
    for g in range(groups):
        t = step * groups + g
        e0 = jnp.maximum(picks_ref[t * PICK + 2], 0)
        e1 = jnp.maximum(picks_ref[t * PICK + 3], 0)
        kx = jnp.concatenate([block_of(ik_ref, e0), block_of(ik_ref, e1)], axis=0)
        iq_g = iq_ref[pl.ds(g * heads, heads), :]
        gate = gate_ref[pl.ds(g * heads, heads), :]
        w = weight_column(wt, t)
        d_logit = d_logit_all[g : g + 1]
        small = jnp.exp(-jnp.abs(gate))
        denom = 1.0 + small
        soft_gate = jnp.maximum(gate, 0.0) + jnp.log(denom)
        sig = jnp.where(gate >= 0.0, 1.0, small) / denom
        dw = jnp.sum(d_logit * soft_gate, axis=1, keepdims=True) * inv_root
        dwt = jnp.where(lane == t, dw, dwt)
        d_gate = (d_logit * (w * inv_root) * sig).astype(jnp.bfloat16)
        gx = d_gate[:, 2 * BLOCK :]
        dx_list.append(dot(gx, kx, 1, 0))
        upd = dot(gx, iq_g, 0, 0)
        acc[e0] += upd[:BLOCK]
        acc[e1] += upd[BLOCK:]
        dg_list.append(d_gate[:, : 2 * BLOCK])
    dwt_ref[...] = dwt
    dg_sh = jnp.concatenate(dg_list, axis=0)
    diq = dot(dg_sh, ksh, 1, 0) + jnp.concatenate(dx_list, axis=0)
    diq_ref[...] = diq.astype(jnp.bfloat16)
    acc_sh[...] += dot(dg_sh, iq_ref[...], 0, 0)

    @pl.when(step == pl.num_programs(0) - 1)
    def _():
        acc[own] += acc_sh[pl.ds(0, BLOCK), :]
        acc[0] += acc_sh[pl.ds(BLOCK, BLOCK), :]
        dik_ref[...] = acc[...].astype(jnp.bfloat16)


def index_logits_call(picks, own, iq, wt, gathered, heads, tokens):
    groups = G_IDX
    span = PICK * BLOCK
    return pl.pallas_call(
        functools.partial(index_logits_kernel, groups, heads),
        grid_spec=pltpu.PrefetchScalarGridSpec(
            num_scalar_prefetch=2,
            grid=(tokens // groups,),
            in_specs=[
                pl.BlockSpec((groups * heads, iq.shape[1]), lambda i, *_: (i, 0)),
                pl.BlockSpec(wt.shape, lambda i, *_: (0, 0)),
                pl.BlockSpec((gathered.shape[0], HALF, LANES), lambda i, *_: (0, 0, 0)),
            ],
            out_specs=[
                pl.BlockSpec((groups * heads, span), lambda i, *_: (i, 0)),
                pl.BlockSpec((groups, span), lambda i, *_: (i, 0)),
            ],
        ),
        out_shape=[
            jax.ShapeDtypeStruct((tokens * heads, span), jnp.float32),
            jax.ShapeDtypeStruct((tokens, span), jnp.float32),
        ],
        compiler_params=pltpu.CompilerParams(vmem_limit_bytes=VMEM_LIMIT),
        cost_estimate=pl.CostEstimate(
            flops=10_000_000_000, bytes_accessed=4_000_000, transcendentals=6_000_000
        ),
        name="index_logits",
    )(picks, own, iq, wt, gathered)


def index_back_call(picks, own, iq, wt, gathered, gate, logits, target, heads, tokens):
    groups = G_IDX
    span = PICK * BLOCK
    width = iq.shape[1]
    nblk = gathered.shape[0] // 2
    return pl.pallas_call(
        functools.partial(index_back_kernel, groups, heads),
        grid_spec=pltpu.PrefetchScalarGridSpec(
            num_scalar_prefetch=2,
            grid=(tokens // groups,),
            in_specs=[
                pl.BlockSpec((groups * heads, width), lambda i, *_: (i, 0)),
                pl.BlockSpec(wt.shape, lambda i, *_: (0, 0)),
                pl.BlockSpec((gathered.shape[0], HALF, LANES), lambda i, *_: (0, 0, 0)),
                pl.BlockSpec((groups * heads, span), lambda i, *_: (i, 0)),
                pl.BlockSpec((groups, span), lambda i, *_: (i, 0)),
                pl.BlockSpec((groups, span), lambda i, *_: (i, 0)),
            ],
            out_specs=[
                pl.BlockSpec((groups * heads, width), lambda i, *_: (i, 0)),
                pl.BlockSpec((heads, tokens), lambda i, *_: (0, 0)),
                pl.BlockSpec((nblk, BLOCK, width), lambda i, *_: (0, 0, 0)),
            ],
            scratch_shapes=[
                pltpu.VMEM((nblk, BLOCK, width), jnp.float32),
                pltpu.VMEM((2 * BLOCK, width), jnp.float32),
            ],
        ),
        out_shape=[
            jax.ShapeDtypeStruct((tokens * heads, width), jnp.bfloat16),
            jax.ShapeDtypeStruct((heads, tokens), jnp.float32),
            jax.ShapeDtypeStruct((nblk, BLOCK, width), jnp.bfloat16),
        ],
        compiler_params=pltpu.CompilerParams(vmem_limit_bytes=VMEM_LIMIT),
        cost_estimate=pl.CostEstimate(
            flops=20_000_000_000, bytes_accessed=8_000_000, transcendentals=6_000_000
        ),
        name="index_back",
    )(picks, own, iq, wt, gathered, gate, logits, target)


def tile_lists(picks):
    nblk = 64
    block = jnp.maximum(picks[:, 2:], 0).reshape(-1)
    npairs = block.shape[0]
    ntiles = -(-(npairs // PAIRS + nblk) // UNROLL) * UNROLL
    hot = (block[:, None] == jnp.arange(nblk)[None, :]).astype(jnp.int32)
    order = jnp.arange(npairs)
    same = (block[:, None] == block[None, :]) & (order[:, None] > order[None, :])
    rank = jnp.sum(same.astype(jnp.int32), axis=1)
    count = jnp.sum(hot, axis=0)
    padded = (count + PAIRS - 1) // PAIRS * PAIRS
    b = jnp.arange(nblk)
    start = jnp.sum(jnp.where(b[None, :] < b[:, None], padded[None, :], 0), axis=1)
    place = jnp.sum(hot * start[None, :], axis=1) + rank
    slots = jnp.arange(ntiles * PAIRS)
    found = place[None, :] == slots[:, None]
    pairs = jnp.sum(jnp.where(found, order[None, :] - npairs, 0), axis=1) + npairs
    ends = start + padded
    tile = jnp.arange(ntiles) * PAIRS
    owner = jnp.sum((ends[None, :] <= tile[:, None]).astype(jnp.int32), axis=1)
    owner = jnp.minimum(owner, nblk - 1)
    steps = (jnp.sum(padded) // PAIRS + UNROLL - 1) // UNROLL
    tiles = jnp.concatenate([steps.reshape(1), owner])
    return tiles.astype(jnp.int32), pairs.astype(jnp.int32)


def swap_heads(x):
    return lax.ppermute(x, "head", [(0, 1), (1, 0)])


def head_sum(x):
    return x + swap_heads(x)


def add_parts(parts):
    return jnp.sum(parts.astype(jnp.float32), axis=0).astype(parts.dtype)


def gather_by_exchange(x, core):
    mine = lax.all_to_all(jnp.broadcast_to(x[None], (64,) + x.shape), "seq", 0, 0, tiled=True)
    other = swap_heads(mine)
    first = jnp.where(core == 0, mine, other)
    second = jnp.where(core == 0, other, mine)
    return jnp.stack([first, second], axis=1).reshape((-1,) + x.shape)


def join_halves(x, core):
    other = swap_heads(x)
    first = jnp.where(core == 0, x, other)
    second = jnp.where(core == 0, other, x)
    return jnp.concatenate([first, second], axis=0)


def pack_half(x):
    full = x.shape[1] // LANES
    tiles = x[:, : full * LANES].reshape(HALF, full, LANES).transpose(1, 0, 2).reshape(-1, LANES)
    last = x[:, full * LANES :]
    return jnp.concatenate([tiles, jnp.concatenate([last[: HALF // 2], last[HALF // 2 :]], axis=1)], axis=0)


def unpack_half(x):
    full = x.shape[0] // HALF
    tiles = x[: full * HALF].reshape(full, HALF, LANES).transpose(1, 0, 2).reshape(HALF, -1)
    last = x[full * HALF :]
    last = jnp.concatenate([last[:, :HALF], last[:, HALF:]], axis=0)
    return jnp.concatenate([tiles, last], axis=1)


def per_device(queries, latent, d_out, index_q, index_w, index_k, picks):
    rows, heads, width = queries.shape
    vwidth = d_out.shape[2]
    iheads, iwidth = index_q.shape[1:]
    wide = -(-width // LANES) * LANES
    core = lax.axis_index("head").astype(jnp.int32)
    own = jnp.stack([lax.axis_index("seq").astype(jnp.int32), core])
    picks_flat = picks.reshape(-1)

    lat_half = lax.dynamic_slice_in_dim(latent, core * HALF, HALF, 0)
    ik_half = lax.dynamic_slice_in_dim(index_k, core * HALF, HALF, 0)
    gathered = lax.all_gather(pack_half(lat_half), ("seq", "head"), axis=0, tiled=False)
    ik_all = gather_by_exchange(ik_half, core)

    iq = index_q.reshape(rows * iheads, iwidth)
    wt = index_w.astype(jnp.float32).T
    gate, logit_part = index_logits_call(picks_flat, own, iq, wt, ik_all, iheads, rows)

    tiles, pairs = tile_lists(picks)
    stk = jnp.concatenate(
        [
            jnp.pad(queries, ((0, 0), (0, 0), (0, wide - width))),
            jnp.pad(d_out, ((0, 0), (0, 0), (0, wide - vwidth))),
        ],
        axis=1,
    )
    own_next, logit_part = lax.optimization_barrier((own, logit_part))
    dsx, dsh, target_part, keep, send = attend_call(picks_flat, own_next, tiles, pairs, stk, gathered, heads)
    lat_part = keep + swap_heads(send)
    target_part, lat_part = lax.optimization_barrier((target_part, lat_part))
    lat_parts = lax.all_to_all(lat_part, "seq", 0, 0, tiled=True)
    target = head_sum(target_part)
    logits = head_sum(logit_part)
    diq, dwt, dik = index_back_call(
        picks_flat, own, iq, wt, ik_all, gate, logits, target, iheads, rows
    )
    dik = dik.reshape(-1, 2, HALF, iwidth)
    ik_keep = lax.dynamic_index_in_dim(dik, core, 1, keepdims=False)
    ik_send = lax.dynamic_index_in_dim(dik, 1 - core, 1, keepdims=False)
    ik_part = ik_keep + swap_heads(ik_send)
    own_late, ik_part = lax.optimization_barrier((own, ik_part))
    dq = query_grad_call(own_late, tiles, pairs, dsx, dsh, gathered, heads, wide)
    dq = dq.reshape(rows, heads, wide)[:, :, :width].transpose(1, 2, 0)
    dq, ik_part, lat_parts = lax.optimization_barrier((dq, ik_part, lat_parts))
    ik_parts = lax.all_to_all(ik_part, "seq", 0, 0, tiled=True)
    lat_sum = add_parts(lat_parts)
    ik_sum = add_parts(ik_parts)

    d_latent = join_halves(unpack_half(lat_sum), core)
    d_index_k = join_halves(ik_sum, core)
    d_queries = dq.transpose(2, 0, 1)
    return (d_queries, d_latent, diq.reshape(rows, iheads, iwidth), dwt.T, d_index_k)


def solution(mesh):
    return jax.shard_map(
        per_device,
        mesh=mesh,
        in_specs=(
            P("seq", "head", None),
            P("seq", None),
            P("seq", "head", None),
            P("seq", "head", None),
            P("seq", "head"),
            P("seq", None),
            P("seq", None),
        ),
        out_specs=(
            P("seq", "head", None),
            P("seq", None),
            P("seq", "head", None),
            P("seq", "head"),
            P("seq", None),
        ),
        check_vma=False,
    )
```

```python
import functools

import jax
import jax.numpy as jnp
from jax import lax
from jax.experimental import pallas as pl
from jax.experimental.pallas import tpu as pltpu
from jax.sharding import PartitionSpec as P

BLOCK = 128
PICK = 4
H = 80
IH = 64
LANES = 128

softmax_scale = 192.0 ** (-0.5)
kl_weight = 32.0
neg_large = -1e30
inv_root = IH ** (-0.5)

G_ATT = 16
G_IDX = 8
UNROLL = 8
PAIRS = 4
HALF = BLOCK // 2
VMEM_LIMIT = 60 * 1024 * 1024


def dot(a, b, ca, cb):
    return lax.dot_general(a, b, (((ca,), (cb,)), ((), ())), preferred_element_type=jnp.float32)


def mask_row(picks_ref, t, tloc):
    lane = lax.broadcasted_iota(jnp.int32, (1, LANES), 1)
    parts = [jnp.where(lane <= tloc, 0.0, neg_large)]
    for j in range(1, PICK):
        parts.append(jnp.where(lane + picks_ref[t * PICK + j] * LANES >= 0, 0.0, neg_large))
    return jnp.concatenate(parts, axis=1)


def block_of(keys, b):
    return keys[pl.ds(2 * b, 2)].reshape(BLOCK, keys.shape[2])


def load_keys(lat_ref, keys, tails, sem):
    full = keys.shape[2] // LANES - 1
    copies = [
        pltpu.make_async_copy(
            lat_ref.at[:, pl.ds(c * HALF, HALF), :],
            keys.at[:, :, pl.ds(c * LANES, LANES)],
            sem.at[c],
        )
        for c in range(full)
    ]
    copies.append(
        pltpu.make_async_copy(
            lat_ref.at[:, pl.ds(full * HALF, HALF // 2), :], tails, sem.at[full]
        )
    )
    for cp in copies:
        cp.start()

    def finish():
        for cp in copies:
            cp.wait()

        def unpack(i, carry):
            low = tails[i]
            high = pltpu.roll(low.astype(jnp.float32), HALF, 1).astype(jnp.bfloat16)
            keys[i, :, pl.ds(full * LANES, LANES)] = jnp.concatenate([low, high], axis=0)
            return carry

        lax.fori_loop(0, keys.shape[0], unpack, 0, unroll=8)

    return finish


def attend_kernel(
    groups, heads, picks_ref, own_ref, tile_ref, pair_ref, stk_hbm, lat_ref,
    dsx_ref, dsh_ref, tgt_ref, keep_ref, send_ref,
    keys, tails, stk, extra, acc, acc_sh, sem,
):
    step = pl.program_id(0)
    own = own_ref[0]
    core = own_ref[1]
    rows = 2 * heads
    nblk = acc.shape[0]
    tokens = stk.shape[0]
    full = keys.shape[2] // LANES - 1

    @pl.when(step == 0)
    def _():
        chunk = tokens // full
        load_stk = [
            pltpu.make_async_copy(
                stk_hbm.at[pl.ds(c * chunk, chunk)], stk.at[pl.ds(c * chunk, chunk)], sem.at[full + 1 + c]
            )
            for c in range(full)
        ]
        finish = load_keys(lat_ref, keys, tails, sem)
        for cp in load_stk:
            cp.start()

        def zero(b, carry):
            acc[b] = jnp.zeros(acc.shape[1:], jnp.float32)
            return carry

        lax.fori_loop(0, nblk, zero, 0)
        acc_sh[...] = jnp.zeros(acc_sh.shape, jnp.float32)
        finish()
        for cp in load_stk:
            cp.wait()

        def tile_pair(i, carry):
            for u in range(UNROLL):
                tile = UNROLL * i + u
                pairs = [pair_ref[tile * PAIRS + k] for k in range(PAIRS)]
                lhs = jnp.concatenate([stk[jnp.minimum(p // 2, tokens - 1)] for p in pairs], axis=0)
                out = dot(lhs, block_of(keys, tile_ref[1 + tile]), 1, 1)
                for k, p in enumerate(pairs):
                    extra[p] = out[k * rows : (k + 1) * rows]
            return carry

        lax.fori_loop(0, tile_ref[0], tile_pair, 0)

    ksh = jnp.concatenate([block_of(keys, own), block_of(keys, 0)], axis=0)
    stk_all = stk[pl.ds(step * groups, groups)].reshape(groups * rows, stk.shape[2])
    both_sh = dot(stk_all, ksh, 1, 1)
    ds_list, gr_list, tgt_list = [], [], []
    for g in range(groups):
        t = step * groups + g
        e0 = jnp.maximum(picks_ref[t * PICK + 2], 0)
        e1 = jnp.maximum(picks_ref[t * PICK + 3], 0)
        bias = mask_row(picks_ref, t, t)
        both_x = jnp.concatenate([extra[2 * t], extra[2 * t + 1]], axis=1)
        lo = g * rows
        scores = jnp.concatenate([both_sh[lo : lo + heads], both_x[:heads]], axis=1)
        dprob = jnp.concatenate([both_sh[lo + heads : lo + rows], both_x[heads:]], axis=1)
        scores = scores * softmax_scale + bias
        top = jnp.max(scores, axis=1, keepdims=True)
        expo = jnp.exp(scores - top)
        probs = expo * (1.0 / jnp.sum(expo, axis=1, keepdims=True))
        delta = jnp.sum(probs * dprob, axis=1, keepdims=True)
        dscore = probs * (dprob - delta) * softmax_scale
        tgt_list.append(jnp.sum(probs, axis=0, keepdims=True))
        grads = jnp.concatenate([dscore, probs], axis=0).astype(jnp.bfloat16)
        dsx_ref[2 * g] = dscore[:, 2 * BLOCK : 3 * BLOCK]
        dsx_ref[2 * g + 1] = dscore[:, 3 * BLOCK :]
        upd = dot(grads[:, 2 * BLOCK :], stk[t], 0, 0)
        acc[e0] += upd[:BLOCK]
        acc[e1] += upd[BLOCK:]
        ds_list.append(dscore[:, : 2 * BLOCK])
        gr_list.append(grads[:, : 2 * BLOCK])
    dsh_ref[...] = jnp.concatenate(ds_list, axis=0).astype(jnp.bfloat16)
    acc_sh[...] += dot(jnp.concatenate(gr_list, axis=0), stk_all, 0, 0)
    tgt_ref[...] = jnp.concatenate(tgt_list, axis=0)

    @pl.when(step == pl.num_programs(0) - 1)
    def _():
        acc[own] += acc_sh[pl.ds(0, BLOCK), :]
        acc[0] += acc_sh[pl.ds(BLOCK, BLOCK), :]

        stores = []
        for k, ref, which in ((0, send_ref, 1 - core), (1, keep_ref, core)):
            rows_of = pl.ds(pl.multiple_of(which * HALF, HALF), HALF)
            part = pl.ds(k * nblk, nblk)

            def cast(b, carry):
                half = acc[b, rows_of, :]
                keys[k * nblk + b] = half.astype(jnp.bfloat16)
                last = half[:, full * LANES :]
                packed = last[: HALF // 2] + pltpu.roll(last[HALF // 2 :], HALF, 1)
                tails[k * nblk + b] = packed.astype(jnp.bfloat16)
                return carry

            lax.fori_loop(0, nblk, cast, 0, unroll=4)
            sent = [
                pltpu.make_async_copy(
                    keys.at[part, :, pl.ds(c * LANES, LANES)],
                    ref.at[:, pl.ds(c * HALF, HALF), :],
                    sem.at[k * (full + 1) + c],
                )
                for c in range(full)
            ]
            sent.append(
                pltpu.make_async_copy(
                    tails.at[part],
                    ref.at[:, pl.ds(full * HALF, HALF // 2), :],
                    sem.at[k * (full + 1) + full],
                )
            )
            for cp in sent:
                cp.start()
            stores += sent
        for cp in stores:
            cp.wait()


def attend_call(picks, own, tiles, pairs, stk, gathered, heads):
    tokens, rows, width = stk.shape
    nblk = gathered.shape[0] // 2
    full = width // LANES - 1
    groups = G_ATT
    packed = full * HALF + HALF // 2
    return pl.pallas_call(
        functools.partial(attend_kernel, groups, heads),
        grid_spec=pltpu.PrefetchScalarGridSpec(
            num_scalar_prefetch=4,
            grid=(tokens // groups,),
            in_specs=[pl.BlockSpec(memory_space=pl.ANY)] * 2,
            out_specs=[
                pl.BlockSpec((2 * groups, heads, BLOCK), lambda i, *_: (i, 0, 0)),
                pl.BlockSpec((groups * heads, 2 * BLOCK), lambda i, *_: (i, 0)),
                pl.BlockSpec((groups, PICK * BLOCK), lambda i, *_: (i, 0)),
                pl.BlockSpec(memory_space=pl.ANY),
                pl.BlockSpec(memory_space=pl.ANY),
            ],
            scratch_shapes=[
                pltpu.VMEM((2 * nblk, HALF, width), jnp.bfloat16),
                pltpu.VMEM((2 * nblk, HALF // 2, LANES), jnp.bfloat16),
                pltpu.VMEM((tokens, rows, width), jnp.bfloat16),
                pltpu.VMEM((2 * tokens + 1, rows, BLOCK), jnp.float32),
                pltpu.VMEM((nblk, BLOCK, width), jnp.float32),
                pltpu.VMEM((2 * BLOCK, width), jnp.float32),
                pltpu.SemaphoreType.DMA((2 * full + 2,)),
            ],
        ),
        out_shape=[
            jax.ShapeDtypeStruct((2 * tokens, heads, BLOCK), jnp.float32),
            jax.ShapeDtypeStruct((tokens * heads, 2 * BLOCK), jnp.bfloat16),
            jax.ShapeDtypeStruct((tokens, PICK * BLOCK), jnp.float32),
            jax.ShapeDtypeStruct((nblk, packed, LANES), jnp.bfloat16),
            jax.ShapeDtypeStruct((nblk, packed, LANES), jnp.bfloat16),
        ],
        compiler_params=pltpu.CompilerParams(vmem_limit_bytes=VMEM_LIMIT),
        cost_estimate=pl.CostEstimate(
            flops=60_000_000_000, bytes_accessed=50_000_000, transcendentals=3_000_000
        ),
        name="attend",
    )(picks, own, tiles, pairs, stk, gathered)


def query_grad_kernel(groups, heads, own_ref, tile_ref, pair_ref, dsx_ref, dsh_ref, lat_ref, dq_ref, keys, tails, total, sem):
    own = own_ref[0]
    npairs = dsx_ref.shape[0]
    width = keys.shape[2]
    finish = load_keys(lat_ref, keys, tails, sem)

    def zero(t, carry):
        total[t] = jnp.zeros(total.shape[1:], jnp.float32)
        return carry

    lax.fori_loop(0, total.shape[0], zero, 0)
    finish()

    def tile_pair(i, carry):
        for u in range(UNROLL):
            tile = UNROLL * i + u
            pairs = [pair_ref[tile * PAIRS + k] for k in range(PAIRS)]
            lhs = jnp.concatenate([dsx_ref[jnp.minimum(p, npairs - 1)] for p in pairs], axis=0)
            out = dot(lhs.astype(jnp.bfloat16), block_of(keys, tile_ref[1 + tile]), 1, 0)
            for k, p in enumerate(pairs):
                total[p // 2] += out[k * heads : (k + 1) * heads]
        return carry

    lax.fori_loop(0, tile_ref[0], tile_pair, 0)
    ksh = jnp.concatenate([block_of(keys, own), block_of(keys, 0)], axis=0)

    def shared(i, carry):
        part = pl.ds(pl.multiple_of(i * groups * heads, groups * heads), groups * heads)
        out = dot(dsh_ref[part, :], ksh, 1, 0)
        out = out + total[pl.ds(i * groups, groups)].reshape(groups * heads, width)
        dq_ref[part, :] = out.astype(jnp.bfloat16)
        return carry

    lax.fori_loop(0, dsh_ref.shape[0] // (groups * heads), shared, 0)


def query_grad_call(own, tiles, pairs, dsx, dsh, gathered, heads, width):
    tokens = dsx.shape[0] // 2
    nblk = gathered.shape[0] // 2
    full = width // LANES - 1
    vmem = pl.BlockSpec(memory_space=pltpu.VMEM)
    smem = pl.BlockSpec(memory_space=pltpu.SMEM)
    return pl.pallas_call(
        functools.partial(query_grad_kernel, 8, heads),
        in_specs=[smem, smem, smem, vmem, vmem, pl.BlockSpec(memory_space=pl.ANY)],
        out_specs=vmem,
        out_shape=jax.ShapeDtypeStruct((tokens * heads, width), jnp.bfloat16),
        scratch_shapes=[
            pltpu.VMEM((2 * nblk, HALF, width), jnp.bfloat16),
            pltpu.VMEM((2 * nblk, HALF // 2, LANES), jnp.bfloat16),
            pltpu.VMEM((tokens + 1, heads, width), jnp.float32),
            pltpu.SemaphoreType.DMA((full + 1,)),
        ],
        compiler_params=pltpu.CompilerParams(vmem_limit_bytes=VMEM_LIMIT),
        cost_estimate=pl.CostEstimate(
            flops=12_000_000_000, bytes_accessed=25_000_000, transcendentals=0
        ),
        name="query_grad",
    )(own, tiles, pairs, dsx, dsh, gathered)


def softplus(x):
    return jnp.maximum(x, 0.0) + jnp.log(1.0 + jnp.exp(-jnp.abs(x)))


def weight_column(wt, t):
    lane = lax.broadcasted_iota(jnp.int32, wt.shape, 1)
    return jnp.sum(jnp.where(lane == t, wt, 0.0), axis=1, keepdims=True)


def index_logits_kernel(groups, heads, picks_ref, own_ref, iq_ref, wt_ref, ik_ref, gate_ref, out_ref):
    step = pl.program_id(0)
    own = own_ref[0]
    ksh = jnp.concatenate([block_of(ik_ref, own), block_of(ik_ref, 0)], axis=0)
    gate_sh = dot(iq_ref[...], ksh, 1, 1)
    wt = wt_ref[...]
    outs = []
    for g in range(groups):
        t = step * groups + g
        e0 = jnp.maximum(picks_ref[t * PICK + 2], 0)
        e1 = jnp.maximum(picks_ref[t * PICK + 3], 0)
        kx = jnp.concatenate([block_of(ik_ref, e0), block_of(ik_ref, e1)], axis=0)
        gate_x = dot(iq_ref[pl.ds(g * heads, heads), :], kx, 1, 1)
        gate = jnp.concatenate([gate_sh[g * heads : (g + 1) * heads], gate_x], axis=1)
        gate_ref[pl.ds(g * heads, heads), :] = gate
        w = weight_column(wt, t)
        outs.append(jnp.sum(w * softplus(gate), axis=0, keepdims=True))
    out_ref[...] = jnp.concatenate(outs, axis=0) * inv_root


def index_back_kernel(
    groups, heads, picks_ref, own_ref, iq_ref, wt_ref, ik_ref, gate_ref, logit_ref, tgt_ref, diq_ref, dwt_ref, dik_ref, acc, acc_sh
):
    step = pl.program_id(0)
    own = own_ref[0]

    @pl.when(step == 0)
    def _():
        acc[...] = jnp.zeros(acc.shape, jnp.float32)
        acc_sh[...] = jnp.zeros(acc_sh.shape, jnp.float32)
        dwt_ref[...] = jnp.zeros(dwt_ref.shape, jnp.float32)

    bias = jnp.concatenate(
        [mask_row(picks_ref, step * groups + g, step * groups + g) for g in range(groups)], axis=0
    )
    logits = logit_ref[...] + bias
    top = jnp.max(logits, axis=1, keepdims=True)
    expo = jnp.exp(logits - top)
    soft = expo * (1.0 / jnp.sum(expo, axis=1, keepdims=True))
    d_logit_all = jnp.where(bias == 0.0, kl_weight * (soft - tgt_ref[...] * (1.0 / H)), 0.0)

    ksh = jnp.concatenate([block_of(ik_ref, own), block_of(ik_ref, 0)], axis=0)
    wt = wt_ref[...]
    lane = lax.broadcasted_iota(jnp.int32, wt.shape, 1)
    dwt = dwt_ref[...]
    dg_list, dx_list = [], []
    for g in range(groups):
        t = step * groups + g
        e0 = jnp.maximum(picks_ref[t * PICK + 2], 0)
        e1 = jnp.maximum(picks_ref[t * PICK + 3], 0)
        kx = jnp.concatenate([block_of(ik_ref, e0), block_of(ik_ref, e1)], axis=0)
        iq_g = iq_ref[pl.ds(g * heads, heads), :]
        gate = gate_ref[pl.ds(g * heads, heads), :]
        w = weight_column(wt, t)
        d_logit = d_logit_all[g : g + 1]
        small = jnp.exp(-jnp.abs(gate))
        denom = 1.0 + small
        soft_gate = jnp.maximum(gate, 0.0) + jnp.log(denom)
        sig = jnp.where(gate >= 0.0, 1.0, small) / denom
        dw = jnp.sum(d_logit * soft_gate, axis=1, keepdims=True) * inv_root
        dwt = jnp.where(lane == t, dw, dwt)
        d_gate = (d_logit * (w * inv_root) * sig).astype(jnp.bfloat16)
        gx = d_gate[:, 2 * BLOCK :]
        dx_list.append(dot(gx, kx, 1, 0))
        upd = dot(gx, iq_g, 0, 0)
        acc[e0] += upd[:BLOCK]
        acc[e1] += upd[BLOCK:]
        dg_list.append(d_gate[:, : 2 * BLOCK])
    dwt_ref[...] = dwt
    dg_sh = jnp.concatenate(dg_list, axis=0)
    diq = dot(dg_sh, ksh, 1, 0) + jnp.concatenate(dx_list, axis=0)
    diq_ref[...] = diq.astype(jnp.bfloat16)
    acc_sh[...] += dot(dg_sh, iq_ref[...], 0, 0)

    @pl.when(step == pl.num_programs(0) - 1)
    def _():
        acc[own] += acc_sh[pl.ds(0, BLOCK), :]
        acc[0] += acc_sh[pl.ds(BLOCK, BLOCK), :]
        dik_ref[...] = acc[...].astype(jnp.bfloat16)


def index_logits_call(picks, own, iq, wt, gathered, heads, tokens):
    groups = G_IDX
    span = PICK * BLOCK
    return pl.pallas_call(
        functools.partial(index_logits_kernel, groups, heads),
        grid_spec=pltpu.PrefetchScalarGridSpec(
            num_scalar_prefetch=2,
            grid=(tokens // groups,),
            in_specs=[
                pl.BlockSpec((groups * heads, iq.shape[1]), lambda i, *_: (i, 0)),
                pl.BlockSpec(wt.shape, lambda i, *_: (0, 0)),
                pl.BlockSpec((gathered.shape[0], HALF, LANES), lambda i, *_: (0, 0, 0)),
            ],
            out_specs=[
                pl.BlockSpec((groups * heads, span), lambda i, *_: (i, 0)),
                pl.BlockSpec((groups, span), lambda i, *_: (i, 0)),
            ],
        ),
        out_shape=[
            jax.ShapeDtypeStruct((tokens * heads, span), jnp.float32),
            jax.ShapeDtypeStruct((tokens, span), jnp.float32),
        ],
        compiler_params=pltpu.CompilerParams(vmem_limit_bytes=VMEM_LIMIT),
        cost_estimate=pl.CostEstimate(
            flops=10_000_000_000, bytes_accessed=4_000_000, transcendentals=6_000_000
        ),
        name="index_logits",
    )(picks, own, iq, wt, gathered)


def index_back_call(picks, own, iq, wt, gathered, gate, logits, target, heads, tokens):
    groups = G_IDX
    span = PICK * BLOCK
    width = iq.shape[1]
    nblk = gathered.shape[0] // 2
    return pl.pallas_call(
        functools.partial(index_back_kernel, groups, heads),
        grid_spec=pltpu.PrefetchScalarGridSpec(
            num_scalar_prefetch=2,
            grid=(tokens // groups,),
            in_specs=[
                pl.BlockSpec((groups * heads, width), lambda i, *_: (i, 0)),
                pl.BlockSpec(wt.shape, lambda i, *_: (0, 0)),
                pl.BlockSpec((gathered.shape[0], HALF, LANES), lambda i, *_: (0, 0, 0)),
                pl.BlockSpec((groups * heads, span), lambda i, *_: (i, 0)),
                pl.BlockSpec((groups, span), lambda i, *_: (i, 0)),
                pl.BlockSpec((groups, span), lambda i, *_: (i, 0)),
            ],
            out_specs=[
                pl.BlockSpec((groups * heads, width), lambda i, *_: (i, 0)),
                pl.BlockSpec((heads, tokens), lambda i, *_: (0, 0)),
                pl.BlockSpec((nblk, BLOCK, width), lambda i, *_: (0, 0, 0)),
            ],
            scratch_shapes=[
                pltpu.VMEM((nblk, BLOCK, width), jnp.float32),
                pltpu.VMEM((2 * BLOCK, width), jnp.float32),
            ],
        ),
        out_shape=[
            jax.ShapeDtypeStruct((tokens * heads, width), jnp.bfloat16),
            jax.ShapeDtypeStruct((heads, tokens), jnp.float32),
            jax.ShapeDtypeStruct((nblk, BLOCK, width), jnp.bfloat16),
        ],
        compiler_params=pltpu.CompilerParams(vmem_limit_bytes=VMEM_LIMIT),
        cost_estimate=pl.CostEstimate(
            flops=20_000_000_000, bytes_accessed=8_000_000, transcendentals=6_000_000
        ),
        name="index_back",
    )(picks, own, iq, wt, gathered, gate, logits, target)


def tile_lists(picks):
    nblk = 64
    block = jnp.maximum(picks[:, 2:], 0).reshape(-1)
    npairs = block.shape[0]
    ntiles = -(-(npairs // PAIRS + nblk) // UNROLL) * UNROLL
    hot = (block[:, None] == jnp.arange(nblk)[None, :]).astype(jnp.int32)
    order = jnp.arange(npairs)
    same = (block[:, None] == block[None, :]) & (order[:, None] > order[None, :])
    rank = jnp.sum(same.astype(jnp.int32), axis=1)
    count = jnp.sum(hot, axis=0)
    padded = (count + PAIRS - 1) // PAIRS * PAIRS
    b = jnp.arange(nblk)
    start = jnp.sum(jnp.where(b[None, :] < b[:, None], padded[None, :], 0), axis=1)
    place = jnp.sum(hot * start[None, :], axis=1) + rank
    slots = jnp.arange(ntiles * PAIRS)
    found = place[None, :] == slots[:, None]
    pairs = jnp.sum(jnp.where(found, order[None, :] - npairs, 0), axis=1) + npairs
    ends = start + padded
    tile = jnp.arange(ntiles) * PAIRS
    owner = jnp.sum((ends[None, :] <= tile[:, None]).astype(jnp.int32), axis=1)
    owner = jnp.minimum(owner, nblk - 1)
    steps = (jnp.sum(padded) // PAIRS + UNROLL - 1) // UNROLL
    tiles = jnp.concatenate([steps.reshape(1), owner])
    return tiles.astype(jnp.int32), pairs.astype(jnp.int32)


def swap_heads(x):
    return lax.ppermute(x, "head", [(0, 1), (1, 0)])


def head_sum(x):
    return x + swap_heads(x)


def add_parts(parts):
    return jnp.sum(parts.astype(jnp.float32), axis=0).astype(parts.dtype)


def gather_by_exchange(x, core):
    mine = lax.all_to_all(jnp.broadcast_to(x[None], (64,) + x.shape), "seq", 0, 0, tiled=True)
    other = swap_heads(mine)
    first = jnp.where(core == 0, mine, other)
    second = jnp.where(core == 0, other, mine)
    return jnp.stack([first, second], axis=1).reshape((-1,) + x.shape)


def join_halves(x, core):
    other = swap_heads(x)
    first = jnp.where(core == 0, x, other)
    second = jnp.where(core == 0, other, x)
    return jnp.concatenate([first, second], axis=0)


def pack_half(x):
    full = x.shape[1] // LANES
    tiles = x[:, : full * LANES].reshape(HALF, full, LANES).transpose(1, 0, 2).reshape(-1, LANES)
    last = x[:, full * LANES :]
    return jnp.concatenate([tiles, jnp.concatenate([last[: HALF // 2], last[HALF // 2 :]], axis=1)], axis=0)


def unpack_half(x):
    full = x.shape[0] // HALF
    tiles = x[: full * HALF].reshape(full, HALF, LANES).transpose(1, 0, 2).reshape(HALF, -1)
    last = x[full * HALF :]
    last = jnp.concatenate([last[:, :HALF], last[:, HALF:]], axis=0)
    return jnp.concatenate([tiles, last], axis=1)


def per_device(queries, latent, d_out, index_q, index_w, index_k, picks):
    rows, heads, width = queries.shape
    vwidth = d_out.shape[2]
    iheads, iwidth = index_q.shape[1:]
    wide = -(-width // LANES) * LANES
    core = lax.axis_index("head").astype(jnp.int32)
    own = jnp.stack([lax.axis_index("seq").astype(jnp.int32), core])
    picks_flat = picks.reshape(-1)

    lat_half = lax.dynamic_slice_in_dim(latent, core * HALF, HALF, 0)
    ik_half = lax.dynamic_slice_in_dim(index_k, core * HALF, HALF, 0)
    gathered = lax.all_gather(pack_half(lat_half), ("seq", "head"), axis=0, tiled=False)
    ik_all = gather_by_exchange(ik_half, core)

    iq = index_q.reshape(rows * iheads, iwidth)
    wt = index_w.astype(jnp.float32).T
    gate, logit_part = index_logits_call(picks_flat, own, iq, wt, ik_all, iheads, rows)

    tiles, pairs = tile_lists(picks)
    stk = jnp.concatenate(
        [
            jnp.pad(queries, ((0, 0), (0, 0), (0, wide - width))),
            jnp.pad(d_out, ((0, 0), (0, 0), (0, wide - vwidth))),
        ],
        axis=1,
    )
    own_next, logit_part = lax.optimization_barrier((own, logit_part))
    dsx, dsh, target_part, keep, send = attend_call(picks_flat, own_next, tiles, pairs, stk, gathered, heads)
    lat_part = keep + swap_heads(send)
    target_part, lat_part = lax.optimization_barrier((target_part, lat_part))
    lat_parts = lax.all_to_all(lat_part, "seq", 0, 0, tiled=True)
    target = head_sum(target_part)
    logits = head_sum(logit_part)
    diq, dwt, dik = index_back_call(
        picks_flat, own, iq, wt, ik_all, gate, logits, target, iheads, rows
    )
    dik = dik.reshape(-1, 2, HALF, iwidth)
    ik_keep = lax.dynamic_index_in_dim(dik, core, 1, keepdims=False)
    ik_send = lax.dynamic_index_in_dim(dik, 1 - core, 1, keepdims=False)
    ik_part = ik_keep + swap_heads(ik_send)
    own_late, ik_part = lax.optimization_barrier((own, ik_part))
    dq = query_grad_call(own_late, tiles, pairs, dsx, dsh, gathered, heads, wide)
    dq = dq.reshape(rows, heads, wide)[:, :, :width].transpose(1, 2, 0)
    dq, ik_part, lat_parts = lax.optimization_barrier((dq, ik_part, lat_parts))
    ik_parts = lax.all_to_all(ik_part, "seq", 0, 0, tiled=True)
    lat_sum = add_parts(lat_parts)
    ik_sum = add_parts(ik_parts)

    d_latent = join_halves(unpack_half(lat_sum), core)
    d_index_k = join_halves(ik_sum, core)
    d_queries = dq.transpose(2, 0, 1)
    return (d_queries, d_latent, diq.reshape(rows, iheads, iwidth), dwt.T, d_index_k)


def solution(mesh):
    return jax.shard_map(
        per_device,
        mesh=mesh,
        in_specs=(
            P("seq", "head", None),
            P("seq", None),
            P("seq", "head", None),
            P("seq", "head", None),
            P("seq", "head"),
            P("seq", None),
            P("seq", None),
        ),
        out_specs=(
            P("seq", "head", None),
            P("seq", None),
            P("seq", "head", None),
            P("seq", "head"),
            P("seq", None),
        ),
        check_vma=False,
    )
```
